512 devices in a mesh: tm: 32 (over z, core), space: 16 (over x, y).
Axes of the slice: x: 4, y: 4, z: 16, core: 2. Of those that a mesh axis runs over, the one named last changes fastest.
Arguments:
- spectrum: float32 [2048], P('space'), may hold values from 4 to 64
- coupling: float32 [256, 2048], P('tm', 'space'), may hold values from 0 to 1, as said below
- spatial_basis: bfloat16 [2048, 2048], P(None, 'space'), may hold values from -0.125 to 0.125
- noise_keys: int32 [64], replicated, may hold values from 0 to 16777215
- noise_counters: int32 [64], replicated, may hold values from 0 to 1048575
Outputs:
- samples: float32 [2048, 16384], P('space', 'tm')
The draws below stay inside these ranges and needn't reach their ends.
Inputs may be any that keep to these rules, and one draw needn't show every extreme that they name: `coupling`: every entry lies strictly between 0 and 1.
All inputs are finite; a program needn't handle non-finite values.
Results may differ from the reference program's by a relative error of at most 0.015.
Values may be sent and summed in bfloat16 or wider, within the bound.
A program may use at most 64 MiB of HBM per device.

```python
import math
import jax
import jax.numpy as jnp
from jax import lax

NODES = 2048
VECS = 64
STEPS_DEV = 8
STEPS = 256


def draw_coupling(key, part):
    streams = jax.random.split(jax.random.fold_in(key, 7), 6)
    slow_share = 0.5
    chosen = jax.random.uniform(streams[0], (NODES,), jnp.float32) < slow_share
    slow_rate = jax.random.uniform(streams[1], (NODES,), jnp.float32, 0.03, 0.1) / STEPS
    fast_rate = jax.random.uniform(streams[2], (NODES,), jnp.float32, 0.045, 0.08)
    baseline_rate = jnp.where(chosen, slow_rate, fast_rate)
    block_cholesky_factor = jnp.exp(0.6931471805599453 * jax.random.uniform(streams[3], (STEPS // STEPS_DEV, 1), jnp.float32))
    block_cholesky_factor = jnp.repeat(block_cholesky_factor, STEPS_DEV, axis=0)
    diagonal_nudge = jax.random.uniform(streams[4], (STEPS, NODES), jnp.float32, 0.7, 1.3)
    places = jax.random.randint(streams[5], (3,), 1, STEPS)
    match_count = jnp.any(jnp.arange(STEPS)[:, None] == places[None, :], axis=1)
    noise_surge = jnp.where(match_count, 0.8, 1.0).astype(jnp.float32)[:, None]
    return (jnp.exp(-baseline_rate[None, :] * block_cholesky_factor * diagonal_nudge) * noise_surge).astype(jnp.float32)


def place_ends(drawn, stream_key, smallest, largest):
    extent = drawn.shape
    place = [jax.random.randint(jax.random.fold_in(stream_key, axis), (), 0, extent[axis]) for axis in range(len(extent))]
    drawn = drawn.at[tuple(place)].set(smallest)
    longest = extent.index(max(extent))
    place[longest] = (place[longest] + 1) % extent[longest]
    return drawn.at[tuple(place)].set(largest)


def steps_of(stream_key, shape, shards, smallest, high):
    def one(position, shards_of):
        draws = jax.random.uniform(jax.random.fold_in(jax.random.fold_in(stream_key, 6), position), (shards_of,), jnp.float32, smallest / len(shards), high / len(shards))
        return jnp.repeat(jnp.exp(draws), shape[position] // shards_of).reshape((-1,) + (1,) * (len(shape) - position - 1))

    factor_of = one(*shards[0])
    for cut in shards[1:]:
        factor_of = factor_of * one(*cut)
    return factor_of


def scatter_about(rng, shape, spread, most, cuts=(), kind=jnp.bfloat16):
    result = spread * jax.random.normal(rng, shape, jnp.float32)
    if cuts:
        result = result * steps_of(rng, shape, cuts, -0.22, 0.18)
    return jnp.clip(result, -most, most).astype(kind)


def setup_inputs(seed: int = 0) -> dict:
    arg_keys = jax.random.split(jax.random.key(seed), 6)
    spectrum = jnp.clip(jnp.exp(math.log(64.0) - 2.7725887 * jax.random.uniform(arg_keys[0], (NODES,), jnp.float32) ** steps_of(arg_keys[0], (NODES,), ((0, 16),), -0.2, 0.2)), 4.0, 64.0)
    coupling = draw_coupling(jax.random.fold_in(arg_keys[5], 71), 0)
    spatial_basis = scatter_about(arg_keys[2], (NODES, NODES), NODES ** -0.5, 0.125, ((1, 16),))
    noise_keys = place_ends(jax.random.randint(arg_keys[3], (VECS,), 0, 16777216), jax.random.fold_in(arg_keys[3], 1), 0, 16777215).astype(jnp.int32)
    noise_counters = place_ends(jax.random.randint(arg_keys[4], (VECS,), 0, 1048576), jax.random.fold_in(arg_keys[4], 1), 0, 1048575).astype(jnp.int32)
    return dict(spectrum=spectrum, coupling=coupling, spatial_basis=spatial_basis, noise_keys=noise_keys, noise_counters=noise_counters)


def mix_bits(state):
    state = state ^ lax.shift_right_logical(state, jnp.int32(16))
    state = state * jnp.int32(-2048144789)
    state = state ^ lax.shift_right_logical(state, jnp.int32(13))
    state = state * jnp.int32(-1028477387)
    state = state ^ lax.shift_right_logical(state, jnp.int32(16))
    return state

def unit_value(state):
    return (lax.shift_right_logical(state, jnp.int32(8)).astype(jnp.float32) + 0.5) * (1.0 / 16777216.0)

def noise_block(noise_keys, noise_counters, step_ids, mode_ids):
    seeded = noise_keys[None, :, None] * jnp.int32(668265261)
    seeded = seeded + (noise_counters[None, :, None] + step_ids[:, None, None]) * jnp.int32(374761393)
    seeded = seeded + mode_ids[None, None, :] * jnp.int32(-1640531535)
    first = mix_bits(seeded)
    second = mix_bits(first + jnp.int32(1013904223))
    radius = jnp.sqrt(-2.0 * jnp.log(unit_value(first)))
    return radius * jnp.cos(6.283185307179586 * unit_value(second))

def reference(spectrum, coupling, spatial_basis, noise_keys, noise_counters):
    step_ids = jnp.arange(STEPS, dtype=jnp.int32)
    mode_ids = jnp.arange(NODES, dtype=jnp.int32)
    noise = noise_block(noise_keys, noise_counters, step_ids, mode_ids)
    diag_part = spectrum[None, :] * (1.0 + coupling * coupling)
    product_part = spectrum[None, :] * coupling
    couple_square = product_part * product_part

    def forward(inverse_matrix, inputs):
        current_diagonal, couple_now = inputs
        pivot = current_diagonal - couple_now * inverse_matrix
        return (1.0 / pivot, pivot)
    _, pivots = lax.scan(forward, jnp.zeros((NODES,), jnp.float32), (diag_part, couple_square))
    scaled = noise / jnp.sqrt(pivots)[:, None, :]

    def backward(carry, inputs):
        scaled_now, pivot, coupling_now = inputs
        value = scaled_now + carry / pivot[None, :]
        return ((spectrum * coupling_now)[None, :] * value, value)
    _, mode_values = lax.scan(backward, jnp.zeros((VECS, NODES), jnp.float32), (scaled, pivots, coupling), reverse=True)
    rounded = mode_values.astype(jnp.bfloat16).reshape(STEPS * VECS, NODES)
    return jnp.dot(spatial_basis, rounded.T, preferred_element_type=jnp.float32)
```

```python
import functools

import jax
import jax.numpy as jnp
from jax import lax
from jax.experimental import pallas as pl
from jax.experimental.pallas import tpu as pltpu
from jax.sharding import PartitionSpec as P

MESH = pl.DeviceIdType.MESH
F32, BF16, I32 = jnp.float32, jnp.bfloat16, jnp.int32
KEY_STEP, TIME_STEP, MODE_STEP = 668265261, 374761393, -1640531535
SINE = (
    6.283185160088995,
    -41.3416550313122,
    81.60100406725992,
    -76.54978216547879,
    39.536705154320686,
)


def mix_bits(h):
    h = h ^ lax.shift_right_logical(h, I32(16))
    h = h * I32(-2048144789)
    h = h ^ lax.shift_right_logical(h, I32(13))
    h = h * I32(-1028477387)
    return h ^ lax.shift_right_logical(h, I32(16))


def noise_of(h):
    first = mix_bits(h)
    second = mix_bits(first + I32(1013904223))
    unit = (lax.shift_right_logical(first, I32(8)).astype(F32) + 0.5) * (1.0 / 16777216.0)
    square = -2.0 * jnp.log(unit)
    radius = square * lax.rsqrt(jnp.maximum(square, 1e-30))
    turn = jnp.abs(lax.shift_right_arithmetic(second, I32(8)).astype(F32) + 0.5)
    y = 0.25 - turn * (1.0 / 16777216.0)
    y2 = y * y
    p = jnp.float32(SINE[-1])
    for c in SINE[-2::-1]:
        p = p * y2 + jnp.float32(c)
    return radius * (p * y)


def shifted(x, by, fill):
    return jnp.concatenate([jnp.full((by, x.shape[1]), fill, F32), x[:-by]], axis=0)


def kernel(
    zt, ns, steps, vecs,
    keys_ref, counters_ref, spec_ref, coup_ref, basis_ref, out_ref,
    base, cz, cs, ps, rows, kin, mine, nz_group, nz_own, omega, last, coef_s, coef_a, vals,
    send, recv, local_sem,
):
    modes = coup_ref.shape[1]
    nodes = basis_ref.shape[0] // ns
    half = vecs // 2
    me_t, me_s = lax.axis_index("tm"), lax.axis_index("space")
    core = lax.rem(me_t, 2)
    chip = me_t // 2
    top = 2 * chip + 1

    barrier = pltpu.get_barrier_semaphore()

    @pl.loop(1, zt)
    def _(j):
        pl.semaphore_signal(
            barrier, inc=1, device_id=(lax.rem(me_t + j, zt), me_s), device_id_type=MESH
        )

    @pl.loop(1, ns)
    def _(j):
        other = lax.rem(me_s + j, ns)
        pl.semaphore_signal(barrier, inc=1, device_id=(me_t, other), device_id_type=MESH)
        pl.semaphore_signal(
            barrier, inc=1, device_id=(me_t + 1 - 2 * core, other), device_id_type=MESH
        )

    lanes = lax.broadcasted_iota(I32, (1, modes), 1) * I32(MODE_STEP)
    for v in range(vecs):
        seed = keys_ref[v] * I32(KEY_STEP) + counters_ref[v] * I32(TIME_STEP)
        base[pl.ds(v, 1), :] = lanes + seed

    first_mode = me_s * modes * I32(MODE_STEP)

    n_group = (zt - top) * (steps // 2)

    def group_noise(lo, hi):
        @pl.loop(lo, hi)
        def _(w):
            seg = zt - 1 - w // (steps // 2)
            i = 2 * lax.rem(w, steps // 2)
            offset = first_mode + (seg * steps + i) * I32(TIME_STEP)
            h = base[pl.ds(pl.multiple_of(core * half, half), half), :] + offset
            nz_group[seg, i] = noise_of(h)
            nz_group[seg, i + 1] = noise_of(h + I32(TIME_STEP))

    def own_noise(lo, hi):
        @pl.loop(lo, hi)
        def _(w):
            block = w // steps
            i = lax.rem(w, steps)
            offset = block * modes * I32(MODE_STEP) + (me_t * steps + i) * I32(TIME_STEP)
            nz_own[block, i] = noise_of(base[...] + offset)

    n_own = ns * steps
    early = jnp.maximum(0, zt // 4 - chip) * 12
    early_group = jnp.minimum(early, n_group)
    group_noise(0, early_group)

    pl.semaphore_wait(barrier, zt - 1 + 2 * (ns - 1))

    def all_copies(count, make):
        @pl.loop(1, count)
        def _(j):
            make(j).start()

    def wait_bytes(ref, sem):
        pltpu.make_async_copy(ref, ref, sem).wait()

    def tile(index):
        return pl.ds(pl.multiple_of(index * steps, steps), steps)

    cz[tile(me_t), :] = coup_ref[...]
    cs[tile(me_s), :] = coup_ref[...]

    def to_line(j):
        return pltpu.make_async_remote_copy(
            src_ref=coup_ref, dst_ref=cz.at[tile(me_t)], send_sem=send.at[0], recv_sem=recv.at[0],
            device_id=(lax.rem(me_t + j, zt), me_s), device_id_type=MESH,
        )

    all_copies(zt, to_line)

    def coupling_to_plane(j):
        return pltpu.make_async_remote_copy(
            src_ref=coup_ref, dst_ref=cs.at[tile(me_s)], send_sem=send.at[1], recv_sem=recv.at[1],
            device_id=(me_t, lax.rem(me_s + j, ns)), device_id_type=MESH,
        )

    all_copies(ns, coupling_to_plane)

    def basis_to_plane(j):
        other = lax.rem(me_s + j, ns)
        return pltpu.make_async_remote_copy(
            src_ref=basis_ref.at[pl.ds(pl.multiple_of(other * nodes, nodes), nodes), :],
            dst_ref=rows.at[me_s], send_sem=send.at[2], recv_sem=recv.at[2],
            device_id=(me_t, other), device_id_type=MESH,
        )

    all_copies(ns, basis_to_plane)
    own_rows = pltpu.make_async_copy(
        basis_ref.at[pl.ds(pl.multiple_of(me_s * nodes, nodes), nodes), :],
        rows.at[me_s],
        local_sem,
    )
    own_rows.start()

    group_noise(early_group, n_group)
    own_noise(0, n_own // 2)

    wait_bytes(cz.at[pl.ds(0, (zt - 1) * steps)], recv.at[0])
    inverse_spec = 1.0 / spec_ref[...]
    c = [cz[pl.ds(i, zt, stride=steps), :] for i in range(steps)]
    alpha, beta = [jnp.ones((zt, modes), F32)], [jnp.zeros((zt, modes), F32)]
    for i in range(steps + 1):
        beta.append(beta[i] + alpha[i])
        if i < steps:
            alpha.append(alpha[i] * (c[i] * c[i]))
    pa, pb = alpha[steps], beta[steps]
    by = 1
    while by < zt:
        pb = shifted(pb, by, 0.0) + shifted(pa, by, 1.0) * pb
        pa = shifted(pa, by, 1.0) * pa
        by *= 2
    pa, pb = shifted(pa, 1, 1.0), shifted(pb, 1, 0.0)
    sums = [pb + pa * beta[i + 1] for i in range(steps + 1)]
    inverse = [1.0 / sums[i + 1] for i in range(steps)]
    keep = [sums[i] * inverse[i] for i in range(steps)]
    gain, weight = jnp.ones((zt, modes), F32), []
    for i in range(steps):
        inner = keep[i] * inverse_spec
        weight.append(gain * c[i] * (inner * lax.rsqrt(inner)))
        gain = gain * (c[i] * keep[i])
    segs = lax.broadcasted_iota(I32, (zt, modes), 0)
    reach = jnp.where(segs > top, gain, 1.0)
    by = 1
    while by < zt:
        reach = shifted(reach, by, 1.0) * reach
        by *= 2
    reach = shifted(reach, 1, 1.0)
    for i in range(steps):
        omega[i] = weight[i] * reach
    last[0] = keep[steps - 1]
    last[1] = gain
    last[2] = pa
    last[3] = pb

    mine[0:1, :] = last[2, pl.ds(me_t, 1), :]
    mine[1:2, :] = last[3, pl.ds(me_t, 1), :]
    mine[2:steps, :] = jnp.broadcast_to(inverse_spec, (steps - 2, modes))
    ps[tile(me_s), :] = mine[...]

    def start_to_plane(j):
        return pltpu.make_async_remote_copy(
            src_ref=mine, dst_ref=ps.at[tile(me_s)], send_sem=send.at[3], recv_sem=recv.at[3],
            device_id=(me_t, lax.rem(me_s + j, ns)), device_id_type=MESH,
        )

    all_copies(ns, start_to_plane)

    def summed(seg, carry):
        terms = [omega[i, pl.ds(seg, 1), :] * nz_group[seg, i] for i in range(steps)]
        while len(terms) > 1:
            terms = [terms[k] + terms[k + 1] for k in range(0, len(terms), 2)]
        return carry + terms[0]

    zero = jnp.zeros((half, modes), F32)
    carry_top = lax.fori_loop(top + 1, zt, summed, zero)
    carry_low = summed(top, last[1, pl.ds(top, 1), :] * carry_top)
    kin_top = (last[0, pl.ds(top, 1), :] * carry_top).astype(BF16)
    kin_low = (last[0, pl.ds(top - 1, 1), :] * carry_low).astype(BF16)
    slot = 2 * me_s + core

    out_low, out_top = kin.at[2 * ns], kin.at[2 * ns + 1]
    out_low[...] = kin_low
    out_top[...] = kin_top

    def low_to_plane(j):
        return pltpu.make_async_remote_copy(
            src_ref=out_low, dst_ref=kin.at[slot], send_sem=send.at[4], recv_sem=recv.at[4],
            device_id=(2 * chip, lax.rem(me_s + j, ns)), device_id_type=MESH,
        )

    def top_to_plane(j):
        return pltpu.make_async_remote_copy(
            src_ref=out_top, dst_ref=kin.at[slot], send_sem=send.at[4], recv_sem=recv.at[4],
            device_id=(top, lax.rem(me_s + j, ns)), device_id_type=MESH,
        )

    all_copies(ns, low_to_plane)
    all_copies(ns, top_to_plane)

    @pl.when(core == 0)
    def _():
        top_to_plane(0).start()
        kin[slot] = kin_low

    @pl.when(core == 1)
    def _():
        low_to_plane(0).start()
        kin[slot] = kin_top

    own_noise(n_own // 2, n_own)

    wait_bytes(cs.at[pl.ds(0, (ns - 1) * steps)], recv.at[1])
    wait_bytes(ps.at[pl.ds(0, (ns - 1) * steps)], recv.at[3])
    c = [cs[pl.ds(i, ns, stride=steps), :] for i in range(steps)]
    pa, pb, inv_s = [ps[pl.ds(i, ns, stride=steps), :] for i in range(3)]
    now = pb + pa
    for i in range(steps):
        pa = pa * (c[i] * c[i])
        after = now + pa
        kept = now / after
        inner = kept * inv_s
        coef_s[i] = inner * lax.rsqrt(inner)
        if i < steps - 1:
            coef_a[i] = kept * c[i + 1]
        now = after

    wait_bytes(rows.at[pl.ds(0, ns - 1)], recv.at[2])
    own_rows.wait()
    wait_bytes(kin.at[pl.ds(0, 2 * ns - 1)], recv.at[4])

    def block_of(b):
        value = jnp.concatenate([kin[2 * b], kin[2 * b + 1]], axis=0).astype(F32)
        for i in range(steps - 1, -1, -1):
            if i < steps - 1:
                value = coef_a[i, pl.ds(b, 1), :] * value
            value = value + coef_s[i, pl.ds(b, 1), :] * nz_own[b, i]
            vals[b, pl.ds(i * vecs, vecs), :] = value.astype(BF16)

    @pl.loop(0, ns)
    def _(b):
        block_of(b)

    def product(b):
        return lax.dot_general(
            rows[b], vals[b], (((1,), (1,)), ((), ())), preferred_element_type=F32
        )

    out_ref[...] = product(0)

    @pl.loop(1, ns)
    def _(b):
        out_ref[...] += product(b)

    wait_bytes(cz.at[pl.ds(0, (zt - 1) * steps)], send.at[0])
    wait_bytes(cs.at[pl.ds(0, (ns - 1) * steps)], send.at[1])
    wait_bytes(rows.at[pl.ds(0, ns - 1)], send.at[2])
    wait_bytes(ps.at[pl.ds(0, (ns - 1) * steps)], send.at[3])
    wait_bytes(kin.at[pl.ds(0, 2 * ns - 1)], send.at[4])


def solution(mesh):
    zt, ns = mesh.shape["tm"], mesh.shape["space"]

    def local(spectrum, coupling, spatial_basis, noise_keys, noise_counters):
        steps, modes = coupling.shape
        vecs = noise_keys.shape[0]
        nodes = spatial_basis.shape[0] // ns
        vmem, smem = pltpu.VMEM, pltpu.SMEM
        return pl.pallas_call(
            functools.partial(kernel, zt, ns, steps, vecs),
            out_shape=jax.ShapeDtypeStruct((nodes, steps * vecs), F32),
            in_specs=[
                pl.BlockSpec(memory_space=smem),
                pl.BlockSpec(memory_space=smem),
                pl.BlockSpec(memory_space=vmem),
                pl.BlockSpec(memory_space=vmem),
                pl.BlockSpec(memory_space=pl.ANY),
            ],
            out_specs=pl.BlockSpec(memory_space=vmem),
            scratch_shapes=[
                vmem((vecs, modes), I32),
                vmem((zt * steps, modes), F32),
                vmem((ns * steps, modes), F32),
                vmem((ns * steps, modes), F32),
                vmem((ns, nodes, modes), BF16),
                vmem((2 * ns + 2, vecs // 2, modes), BF16),
                vmem((steps, modes), F32),
                vmem((zt, steps, vecs // 2, modes), F32),
                vmem((ns, steps, vecs, modes), F32),
                vmem((steps, zt, modes), F32),
                vmem((4, zt, modes), F32),
                vmem((steps, ns, modes), F32),
                vmem((steps, ns, modes), F32),
                vmem((ns, steps * vecs, modes), BF16),
                pltpu.SemaphoreType.DMA((5,)),
                pltpu.SemaphoreType.DMA((5,)),
                pltpu.SemaphoreType.DMA,
            ],
            compiler_params=pltpu.CompilerParams(
                collective_id=0, has_side_effects=True, vmem_limit_bytes=48 * 2**20
            ),
        )(noise_keys, noise_counters, spectrum.reshape(1, modes), coupling, spatial_basis)

    return jax.shard_map(
        local,
        mesh=mesh,
        in_specs=(P("space"), P("tm", "space"), P(None, "space"), P(), P()),
        out_specs=P("space", "tm"),
        check_vma=False,
    )
```

```python
import functools

import jax
import jax.numpy as jnp
from jax import lax
from jax.experimental import pallas as pl
from jax.experimental.pallas import tpu as pltpu
from jax.sharding import PartitionSpec as P

MESH = pl.DeviceIdType.MESH
F32, BF16, I32 = jnp.float32, jnp.bfloat16, jnp.int32
KEY_STEP, TIME_STEP, MODE_STEP = 668265261, 374761393, -1640531535
SINE = (
    6.283185160088995,
    -41.3416550313122,
    81.60100406725992,
    -76.54978216547879,
    39.536705154320686,
)


def mix_bits(h):
    h = h ^ lax.shift_right_logical(h, I32(16))
    h = h * I32(-2048144789)
    h = h ^ lax.shift_right_logical(h, I32(13))
    h = h * I32(-1028477387)
    return h ^ lax.shift_right_logical(h, I32(16))


def noise_of(h):
    first = mix_bits(h)
    second = mix_bits(first + I32(1013904223))
    unit = (lax.shift_right_logical(first, I32(8)).astype(F32) + 0.5) * (1.0 / 16777216.0)
    square = -2.0 * jnp.log(unit)
    radius = square * lax.rsqrt(jnp.maximum(square, 1e-30))
    turn = jnp.abs(lax.shift_right_arithmetic(second, I32(8)).astype(F32) + 0.5)
    y = 0.25 - turn * (1.0 / 16777216.0)
    y2 = y * y
    p = jnp.float32(SINE[-1])
    for c in SINE[-2::-1]:
        p = p * y2 + jnp.float32(c)
    return radius * (p * y)


def shifted(x, by, fill):
    return jnp.concatenate([jnp.full((by, x.shape[1]), fill, F32), x[:-by]], axis=0)


def kernel(
    zt, ns, steps, vecs,
    keys_hbm, counters_hbm, spec_hbm, coup_hbm, basis_ref, out_ref,
    keys_ref, counters_ref, spec_ref, coup_ref, base, cz, cs, ps, rows, kin, mine,
    nz_group, nz_own, omega, above, coef_s, coef_a, vals,
    send, recv, local_sem,
):
    modes = coup_ref.shape[1]
    nodes = basis_ref.shape[0] // ns
    half = vecs // 2
    chips, long = zt // 2, 2 * steps
    me_t, me_s = lax.axis_index("tm"), lax.axis_index("space")
    core = lax.rem(me_t, 2)
    sibling = me_t + 1 - 2 * core
    chip = me_t // 2

    barrier = pltpu.get_barrier_semaphore()

    def greet(t, s):
        pl.semaphore_signal(barrier, inc=1, device_id=(t, s), device_id_type=MESH)

    @pl.loop(1, chips)
    def _(j):
        greet(lax.rem(me_t + 2 * j, zt), me_s)

    greet(sibling, me_s)

    @pl.loop(1, ns)
    def _(j):
        other = lax.rem(me_s + j, ns)
        greet(me_t, other)
        greet(sibling, other)

    loads = [
        pltpu.make_async_copy(src, dst, local_sem.at[k])
        for k, (src, dst) in enumerate(
            [
                (keys_hbm, keys_ref),
                (counters_hbm, counters_ref),
                (spec_hbm, spec_ref),
                (coup_hbm, coup_ref),
                (
                    basis_ref.at[pl.ds(pl.multiple_of(me_s * nodes, nodes), nodes), :],
                    rows.at[me_s],
                ),
            ]
        )
    ]
    for load in loads:
        load.start()
    loads[0].wait()
    loads[1].wait()

    lanes = lax.broadcasted_iota(I32, (1, modes), 1) * I32(MODE_STEP)
    for v in range(vecs):
        seed = keys_ref[v] * I32(KEY_STEP) + counters_ref[v] * I32(TIME_STEP)
        base[pl.ds(v, 1), :] = lanes + seed

    first_mode = me_s * modes * I32(MODE_STEP)

    n_group = (chips - 1 - chip) * steps + steps // 2

    def group_noise(lo, hi):
        @pl.loop(lo, hi)
        def _(w):
            there = chips - 1 - w // steps
            i = 2 * (steps - 1 - lax.rem(w, steps))
            offset = first_mode + (there * long + i) * I32(TIME_STEP)
            h = base[pl.ds(pl.multiple_of(core * half, half), half), :] + offset
            nz_group[there, i] = noise_of(h)
            nz_group[there, i + 1] = noise_of(h + I32(TIME_STEP))

    def own_noise(lo, hi):
        @pl.loop(lo, hi)
        def _(w):
            block = w // steps
            i = lax.rem(w, steps)
            offset = block * modes * I32(MODE_STEP) + (me_t * steps + i) * I32(TIME_STEP)
            nz_own[block, i] = noise_of(base[...] + offset)

    n_own = ns * steps
    early = jnp.where(chip < chips // 2, 200 - 17 * chip, 20)
    late = jnp.where(chip < chips // 2, 0, n_own // 4)
    early_group = jnp.minimum(early, n_group)
    early_own = jnp.minimum(early - early_group, n_own)
    group_noise(0, early_group)
    own_noise(0, early_own)

    def wait_bytes(ref, sem):
        pltpu.make_async_copy(ref, ref, sem).wait()

    def tile(index):
        return pl.ds(pl.multiple_of(index * steps, steps), steps)

    loads[3].wait()
    mine_at = core * chips + chip
    cz[tile(mine_at), :] = coup_ref[...]
    cs[tile(me_s), :] = coup_ref[...]
    pl.semaphore_wait(barrier, chips - 1 + 1 + 2 * (ns - 1))

    @pl.loop(0, chips - 1)
    def _(j):
        to = j + (j >= chip).astype(I32)
        pltpu.make_async_remote_copy(
            src_ref=coup_ref, dst_ref=cz.at[tile(mine_at)], send_sem=send.at[0], recv_sem=recv.at[0],
            device_id=(2 * to + core, me_s), device_id_type=MESH,
        ).start()

    def all_copies(make):
        @pl.loop(1, ns)
        def _(j):
            make(lax.rem(me_s + j, ns)).start()

    def coupling_to_plane(other):
        return pltpu.make_async_remote_copy(
            src_ref=coup_ref, dst_ref=cs.at[tile(me_s)], send_sem=send.at[1], recv_sem=recv.at[1],
            device_id=(me_t, other), device_id_type=MESH,
        )

    all_copies(coupling_to_plane)

    def basis_to_plane(other):
        return pltpu.make_async_remote_copy(
            src_ref=basis_ref.at[pl.ds(pl.multiple_of(other * nodes, nodes), nodes), :],
            dst_ref=rows.at[me_s], send_sem=send.at[2], recv_sem=recv.at[2],
            device_id=(me_t, other), device_id_type=MESH,
        )

    all_copies(basis_to_plane)

    group_noise(early_group, n_group)
    own_noise(early_own, jnp.maximum(early_own, n_own - late))

    wait_bytes(cz.at[pl.ds(0, (chips - 1) * steps)], recv.at[0])
    line = pl.ds(pl.multiple_of(core * chips * steps, steps), chips * steps)
    across = pltpu.make_async_remote_copy(
        src_ref=cz.at[line], dst_ref=cz.at[line], send_sem=send.at[5], recv_sem=recv.at[5],
        device_id=(sibling, me_s), device_id_type=MESH,
    )
    across.start()
    loads[2].wait()
    inverse_spec = 1.0 / spec_ref[...]
    across.wait_recv()

    c = [
        cz[pl.ds(p * chips * steps + i, chips, stride=steps), :]
        for p in range(2)
        for i in range(steps)
    ]
    one, nil = jnp.ones((chips, modes), F32), jnp.zeros((chips, modes), F32)
    alpha, beta = [one], [nil]
    for i in range(long + 1):
        beta.append(beta[i] + alpha[i])
        if i < long:
            alpha.append(alpha[i] * (c[i] * c[i]))
    pa, pb = alpha[long], beta[long]
    by = 1
    while by < chips:
        pb = shifted(pb, by, 0.0) + shifted(pa, by, 1.0) * pb
        pa = shifted(pa, by, 1.0) * pa
        by *= 2
    pa, pb = shifted(pa, 1, 1.0), shifted(pb, 1, 0.0)

    above[0] = jnp.where(core == 0, pa, pa * alpha[steps])
    above[1] = jnp.where(core == 0, pb, pb + pa * beta[steps])
    mine[0:1, :] = above[0, pl.ds(chip, 1), :]
    mine[1:2, :] = above[1, pl.ds(chip, 1), :]
    mine[2:steps, :] = jnp.broadcast_to(inverse_spec, (steps - 2, modes))
    ps[tile(me_s), :] = mine[...]

    def start_to_plane(other):
        return pltpu.make_async_remote_copy(
            src_ref=mine, dst_ref=ps.at[tile(me_s)], send_sem=send.at[3], recv_sem=recv.at[3],
            device_id=(me_t, other), device_id_type=MESH,
        )

    all_copies(start_to_plane)

    sums = [pb + pa * beta[i + 1] for i in range(long + 1)]
    inverse = [1.0 / sums[i + 1] for i in range(long)]
    keep = [sums[i] * inverse[i] for i in range(long)]
    gains, weight = [], []
    for first in (0, steps):
        gain = one
        for i in range(first, first + steps):
            inner = keep[i] * inverse_spec
            weight.append(gain * c[i] * (inner * lax.rsqrt(inner)))
            gain = gain * (c[i] * keep[i])
        gains.append(gain)
    numbers = lax.broadcasted_iota(I32, (chips, modes), 0)
    reach = jnp.where(numbers > chip, gains[0] * gains[1], 1.0)
    by = 1
    while by < chips:
        reach = shifted(reach, by, 1.0) * reach
        by *= 2
    reach = shifted(reach, 1, 1.0)
    middle = reach * gains[0]
    for i in range(steps):
        omega[i] = weight[i] * reach
        omega[steps + i] = weight[steps + i] * middle
        above[5 + i] = weight[steps + i]
    above[2] = keep[long - 1]
    above[3] = keep[steps - 1]
    above[4] = gains[1]

    def added(terms):
        while len(terms) > 1:
            terms = [terms[k] + terms[k + 1] for k in range(0, len(terms), 2)]
        return terms[0]

    def summed(there, carry):
        return carry + added(
            [omega[i, pl.ds(there, 1), :] * nz_group[there, i] for i in range(long)]
        )

    carry_top = lax.fori_loop(chip + 1, chips, summed, jnp.zeros((half, modes), F32))
    carry_low = above[4, pl.ds(chip, 1), :] * carry_top + added(
        [above[5 + i, pl.ds(chip, 1), :] * nz_group[chip, steps + i] for i in range(steps)]
    )
    kin_top = (above[2, pl.ds(chip, 1), :] * carry_top).astype(BF16)
    kin_low = (above[3, pl.ds(chip, 1), :] * carry_low).astype(BF16)
    slot = 2 * me_s + core

    out_low, out_top = kin.at[2 * ns], kin.at[2 * ns + 1]
    out_low[...] = kin_low
    out_top[...] = kin_top

    def low_to_plane(other):
        return pltpu.make_async_remote_copy(
            src_ref=out_low, dst_ref=kin.at[slot], send_sem=send.at[4], recv_sem=recv.at[4],
            device_id=(2 * chip, other), device_id_type=MESH,
        )

    def top_to_plane(other):
        return pltpu.make_async_remote_copy(
            src_ref=out_top, dst_ref=kin.at[slot], send_sem=send.at[4], recv_sem=recv.at[4],
            device_id=(2 * chip + 1, other), device_id_type=MESH,
        )

    all_copies(low_to_plane)
    all_copies(top_to_plane)

    @pl.when(core == 0)
    def _():
        top_to_plane(me_s).start()
        kin[slot] = kin_low

    @pl.when(core == 1)
    def _():
        low_to_plane(me_s).start()
        kin[slot] = kin_top

    own_noise(jnp.maximum(early_own, n_own - late), n_own)

    wait_bytes(cs.at[pl.ds(0, (ns - 1) * steps)], recv.at[1])
    wait_bytes(ps.at[pl.ds(0, (ns - 1) * steps)], recv.at[3])
    c = [cs[pl.ds(i, ns, stride=steps), :] for i in range(steps)]
    pa, pb, inv_s = [ps[pl.ds(i, ns, stride=steps), :] for i in range(3)]
    now = pb + pa
    for i in range(steps):
        pa = pa * (c[i] * c[i])
        after = now + pa
        kept = now / after
        inner = kept * inv_s
        coef_s[i] = inner * lax.rsqrt(inner)
        if i < steps - 1:
            coef_a[i] = kept * c[i + 1]
        now = after

    wait_bytes(rows.at[pl.ds(0, ns - 1)], recv.at[2])
    loads[4].wait()
    wait_bytes(kin.at[pl.ds(0, 2 * ns - 1)], recv.at[4])

    for b in range(ns):
        value = jnp.concatenate([kin[2 * b], kin[2 * b + 1]], axis=0).astype(F32)
        for i in range(steps - 1, -1, -1):
            if i < steps - 1:
                value = coef_a[i, pl.ds(b, 1), :] * value
            value = value + coef_s[i, pl.ds(b, 1), :] * nz_own[b, i]
            vals[b, pl.ds(i * vecs, vecs), :] = value.astype(BF16)
        product = lax.dot_general(
            rows[b], vals[b], (((1,), (1,)), ((), ())), preferred_element_type=F32
        )
        if b == 0:
            out_ref[...] = product
        else:
            out_ref[...] += product

    wait_bytes(cz.at[pl.ds(0, (chips - 1) * steps)], send.at[0])
    wait_bytes(cs.at[pl.ds(0, (ns - 1) * steps)], send.at[1])
    wait_bytes(rows.at[pl.ds(0, ns - 1)], send.at[2])
    wait_bytes(ps.at[pl.ds(0, (ns - 1) * steps)], send.at[3])
    wait_bytes(kin.at[pl.ds(0, 2 * ns - 1)], send.at[4])
    across.wait_send()


def solution(mesh):
    zt, ns = mesh.shape["tm"], mesh.shape["space"]

    def local(spectrum, coupling, spatial_basis, noise_keys, noise_counters):
        steps, modes = coupling.shape
        vecs = noise_keys.shape[0]
        nodes = spatial_basis.shape[0] // ns
        vmem, smem = pltpu.VMEM, pltpu.SMEM
        return pl.pallas_call(
            functools.partial(kernel, zt, ns, steps, vecs),
            out_shape=jax.ShapeDtypeStruct((nodes, steps * vecs), F32),
            in_specs=[pl.BlockSpec(memory_space=pltpu.HBM)] * 5,
            out_specs=pl.BlockSpec(memory_space=vmem),
            scratch_shapes=[
                smem((vecs,), I32),
                smem((vecs,), I32),
                vmem((1, modes), F32),
                vmem((steps, modes), F32),
                vmem((vecs, modes), I32),
                vmem((zt * steps, modes), F32),
                vmem((ns * steps, modes), F32),
                vmem((ns * steps, modes), F32),
                vmem((ns, nodes, modes), BF16),
                vmem((2 * ns + 2, vecs // 2, modes), BF16),
                vmem((steps, modes), F32),
                vmem((zt // 2, 2 * steps, vecs // 2, modes), F32),
                vmem((ns, steps, vecs, modes), F32),
                vmem((2 * steps, zt // 2, modes), F32),
                vmem((5 + steps, zt // 2, modes), F32),
                vmem((steps, ns, modes), F32),
                vmem((steps, ns, modes), F32),
                vmem((ns, steps * vecs, modes), BF16),
                pltpu.SemaphoreType.DMA((6,)),
                pltpu.SemaphoreType.DMA((6,)),
                pltpu.SemaphoreType.DMA((5,)),
            ],
            compiler_params=pltpu.CompilerParams(
                collective_id=0, has_side_effects=True, vmem_limit_bytes=62 * 2**20
            ),
        )(noise_keys, noise_counters, spectrum.reshape(1, modes), coupling, spatial_basis)

    return jax.shard_map(
        local,
        mesh=mesh,
        in_specs=(P("space"), P("tm", "space"), P(None, "space"), P(), P()),
        out_specs=P("space", "tm"),
        check_vma=False,
    )
```

```python
import functools

import jax
import jax.numpy as jnp
from jax import lax
from jax.experimental import pallas as pl
from jax.experimental.pallas import tpu as pltpu
from jax.sharding import PartitionSpec as P

MESH = pl.DeviceIdType.MESH
F32, BF16, I32 = jnp.float32, jnp.bfloat16, jnp.int32
KEY_STEP, TIME_STEP, MODE_STEP = 668265261, 374761393, -1640531535
SINE = (
    6.283185160088995,
    -41.3416550313122,
    81.60100406725992,
    -76.54978216547879,
    39.536705154320686,
)


def mix_bits(h):
    h = h ^ lax.shift_right_logical(h, I32(16))
    h = h * I32(-2048144789)
    h = h ^ lax.shift_right_logical(h, I32(13))
    h = h * I32(-1028477387)
    return h ^ lax.shift_right_logical(h, I32(16))


def noise_of(h):
    first = mix_bits(h)
    second = mix_bits(first + I32(1013904223))
    unit = (lax.shift_right_logical(first, I32(8)).astype(F32) + 0.5) * (1.0 / 16777216.0)
    square = -2.0 * jnp.log(unit)
    radius = square * lax.rsqrt(jnp.maximum(square, 1e-30))
    turn = jnp.abs(lax.shift_right_arithmetic(second, I32(8)).astype(F32) + 0.5)
    y = 0.25 - turn * (1.0 / 16777216.0)
    y2 = y * y
    p = jnp.float32(SINE[-1])
    for c in SINE[-2::-1]:
        p = p * y2 + jnp.float32(c)
    return radius * (p * y)


def shifted(x, by, fill):
    return jnp.concatenate([jnp.full((by, x.shape[1]), fill, F32), x[:-by]], axis=0)


def kernel(
    zt, ns, steps, vecs,
    keys_hbm, counters_hbm, spec_hbm, coup_hbm, basis_ref, out_ref,
    keys_ref, counters_ref, spec_ref, coup_ref, base, fixed, cz, cs, ps, rows, kin, mine,
    nz, omega, above, coef_s, coef_a, vals,
    send, recv, local_sem, meet,
):
    modes = coup_ref.shape[1]
    nodes = basis_ref.shape[0] // ns
    half = vecs // 2
    chips, long = zt // 2, 2 * steps
    me_t, me_s = lax.axis_index("tm"), lax.axis_index("space")
    core = lax.rem(me_t, 2)
    sibling = me_t + 1 - 2 * core
    chip = me_t // 2

    split, outer = chips // 2, chips * 3 // 4
    leading = chip < split
    inner = jnp.logical_and(chip >= split, chip < outer)
    is_hub = chip == split - 1
    line_in, near_in, plane_in, line_go, plane_go = (meet.at[k] for k in range(5))
    barrier = pltpu.get_barrier_semaphore()

    def signal(sem, t, s):
        pl.semaphore_signal(sem, inc=1, device_id=(t, s), device_id_type=MESH)

    def signal_plane(sem):
        signal(sem, sibling, me_s)

        @pl.loop(1, ns)
        def _(j):
            other = lax.rem(me_s + j, ns)
            signal(sem, me_t, other)
            signal(sem, sibling, other)

    @pl.when(leading)
    def _():
        @pl.loop(1, chips)
        def _(j):
            signal(barrier, lax.rem(me_t + 2 * j, zt), me_s)

    @pl.when(jnp.logical_not(inner))
    def _():
        signal_plane(barrier)

    def half_rows(owner):
        start = owner * nodes + core * (nodes // 2)
        return pl.ds(pl.multiple_of(start, nodes // 2), nodes // 2)

    loads = [
        pltpu.make_async_copy(src, dst, local_sem.at[k])
        for k, (src, dst) in enumerate(
            [
                (keys_hbm, keys_ref),
                (counters_hbm, counters_ref),
                (spec_hbm, spec_ref),
                (coup_hbm, coup_ref),
                (basis_ref.at[half_rows(me_s), :], rows.at[core, me_s]),
            ]
        )
    ]
    for load in loads:
        load.start()
    loads[0].wait()
    loads[1].wait()

    lanes = lax.broadcasted_iota(I32, (1, modes), 1) * I32(MODE_STEP)
    for v in range(vecs):
        seed = keys_ref[v] * I32(KEY_STEP) + counters_ref[v] * I32(TIME_STEP)
        base[0, pl.ds(v, 1), :] = lanes + seed

    halved = base[0, pl.ds(pl.multiple_of(core * half, half), half), :]
    base[1, 0:half, :] = halved
    base[1, half:vecs, :] = halved + I32(TIME_STEP)

    n_group = chips - chip
    total = n_group + ns
    limits = [
        jnp.where(leading, 19 - 2 * chip, jnp.maximum(0, chip - split - 3)),
        jnp.where(leading, 22 - 2 * chip, 13),
        jnp.where(leading, 28 - 2 * chip, 18),
        total,
    ]
    limits = [jnp.clip(limit, 0, total - ns // 2) for limit in limits]

    def noise_part(lo, hi):
        @pl.loop(lo, hi)
        def _(u):
            group = u < n_group
            there, block = chips - 1 - u, u - n_group
            start = jnp.where(group, there * long, me_t * steps)
            mode = jnp.where(group, me_s, block) * modes
            offset = mode * I32(MODE_STEP) + start * I32(TIME_STEP)
            stride = jnp.where(group, I32(2 * TIME_STEP), I32(TIME_STEP))
            at = jnp.where(group, there, chips + block) * steps
            kind = jnp.where(group, 1, 0)

            @pl.loop(0, steps)
            def _(i):
                nz[at + i] = noise_of(base[kind] + (offset + i * stride))

    noise_part(0, limits[0])

    def wait_bytes(ref, sem):
        pltpu.make_async_copy(ref, ref, sem).wait()

    def tile(index):
        return pl.ds(pl.multiple_of(index * steps, steps), steps)

    loads[3].wait()
    mine_at = core * chips + chip
    cz[tile(mine_at), :] = coup_ref[...]
    loads[2].wait()
    inverse_spec = 1.0 / spec_ref[...]
    fixed[0:steps, :] = coup_ref[...]
    fixed[steps : 2 * steps, :] = jnp.broadcast_to(inverse_spec, (steps, modes))
    own_fixed = pl.ds(pl.multiple_of(me_s * long, long), long)
    cs[own_fixed, :] = fixed[...]

    def to_chips(lo, hi):
        @pl.loop(lo, hi)
        def _(to):
            @pl.when(to != chip)
            def _():
                pltpu.make_async_remote_copy(
                    src_ref=coup_ref, dst_ref=cz.at[tile(mine_at)],
                    send_sem=send.at[0], recv_sem=recv.at[0],
                    device_id=(2 * to + core, me_s), device_id_type=MESH,
                ).start()

    def all_copies(make):
        @pl.loop(1, ns)
        def _(j):
            make(lax.rem(me_s + j, ns)).start()

    def coupling_to_plane(other):
        return pltpu.make_async_remote_copy(
            src_ref=fixed, dst_ref=cs.at[own_fixed], send_sem=send.at[1], recv_sem=recv.at[1],
            device_id=(me_t, other), device_id_type=MESH,
        )

    def basis_to_plane(other):
        return pltpu.make_async_remote_copy(
            src_ref=basis_ref.at[half_rows(other), :],
            dst_ref=rows.at[core, me_s], send_sem=send.at[2], recv_sem=recv.at[2],
            device_id=(me_t, other), device_id_type=MESH,
        )

    def signal_chips(sem, lo, hi):
        @pl.loop(lo, hi)
        def _(to):
            signal(sem, 2 * to + core, me_s)

    @pl.when(leading)
    def _():
        pl.semaphore_wait(barrier, split - 1 + 1 + 2 * (ns - 1))
        to_chips(0, split)
        all_copies(coupling_to_plane)
        all_copies(basis_to_plane)

    @pl.when(jnp.logical_not(leading))
    def _():
        @pl.when(inner)
        def _():
            pl.semaphore_wait(barrier, split)

        @pl.when(chip >= outer)
        def _():
            pl.semaphore_wait(barrier, split + 1 + 2 * (ns - 1))

        to_chips(0, split)

        @pl.when(inner)
        def _():
            signal(near_in, 2 * (split - 1) + core, me_s)

        signal_chips(line_in, 0, split)

        @pl.when(chip >= outer)
        def _():
            all_copies(coupling_to_plane)
            all_copies(basis_to_plane)

    noise_part(limits[0], limits[1])

    @pl.when(is_hub)
    def _():
        pl.semaphore_wait(near_in, outer - split)
        signal_plane(plane_in)

    @pl.when(inner)
    def _():
        pl.semaphore_wait(plane_go, 1)
        all_copies(coupling_to_plane)
        all_copies(basis_to_plane)

    noise_part(limits[1], limits[2])

    @pl.when(is_hub)
    def _():
        pl.semaphore_wait(plane_in, 1 + 2 * (ns - 1))
        signal_chips(plane_go, split, outer)

    @pl.when(leading)
    def _():
        pl.semaphore_wait(line_in, chips - split)

        @pl.when(chip == 0)
        def _():
            signal_chips(line_go, split, chips)

        to_chips(split, chips)

    @pl.when(jnp.logical_not(leading))
    def _():
        pl.semaphore_wait(line_go, 1)
        to_chips(split, chips)

    noise_part(limits[2], limits[3])

    wait_bytes(cz.at[pl.ds(0, (chips - 1) * steps)], recv.at[0])
    line = pl.ds(pl.multiple_of(core * chips * steps, steps), chips * steps)
    across = pltpu.make_async_remote_copy(
        src_ref=cz.at[line], dst_ref=cz.at[line], send_sem=send.at[5], recv_sem=recv.at[5],
        device_id=(sibling, me_s), device_id_type=MESH,
    )
    across.start()
    across.wait_recv()

    c = [
        cz[pl.ds(p * chips * steps + i, chips, stride=steps), :]
        for p in range(2)
        for i in range(steps)
    ]
    one, nil = jnp.ones((chips, modes), F32), jnp.zeros((chips, modes), F32)
    alpha, beta = [one], [nil]
    for i in range(long + 1):
        beta.append(beta[i] + alpha[i])
        if i < long:
            alpha.append(alpha[i] * (c[i] * c[i]))
    pa, pb = alpha[long], beta[long]
    by = 1
    while by < chips:
        pb = shifted(pb, by, 0.0) + shifted(pa, by, 1.0) * pb
        pa = shifted(pa, by, 1.0) * pa
        by *= 2
    pa, pb = shifted(pa, 1, 1.0), shifted(pb, 1, 0.0)

    above[0] = jnp.where(core == 0, pa, pa * alpha[steps])
    above[1] = jnp.where(core == 0, pb, pb + pa * beta[steps])
    mine[0:1, :] = above[0, pl.ds(chip, 1), :]
    mine[1:2, :] = above[1, pl.ds(chip, 1), :]
    ps[me_s] = mine[...]

    def start_to_plane(other):
        return pltpu.make_async_remote_copy(
            src_ref=mine, dst_ref=ps.at[me_s], send_sem=send.at[3], recv_sem=recv.at[3],
            device_id=(me_t, other), device_id_type=MESH,
        )

    all_copies(start_to_plane)

    sums = [pb + pa * beta[i + 1] for i in range(long + 1)]
    inverse = [1.0 / sums[i + 1] for i in range(long)]
    keep = [sums[i] * inverse[i] for i in range(long)]
    gains, weight = [], []
    for first in (0, steps):
        gain = one
        for i in range(first, first + steps):
            inner = keep[i] * inverse_spec
            weight.append(gain * c[i] * (inner * lax.rsqrt(inner)))
            gain = gain * (c[i] * keep[i])
        gains.append(gain)
    numbers = lax.broadcasted_iota(I32, (chips, modes), 0)
    reach = jnp.where(numbers > chip, gains[0] * gains[1], 1.0)
    by = 1
    while by < chips:
        reach = shifted(reach, by, 1.0) * reach
        by *= 2
    reach = shifted(reach, 1, 1.0)
    middle = reach * gains[0]
    for i in range(steps):
        omega[i] = weight[i] * reach
        omega[steps + i] = weight[steps + i] * middle
        above[5 + i] = weight[steps + i]
    above[2] = keep[long - 1]
    above[3] = keep[steps - 1]
    above[4] = gains[1]

    def added(terms):
        while len(terms) > 1:
            terms = [terms[k] + terms[k + 1] for k in range(0, len(terms), 2)]
        return terms[0]

    def group_at(there, i):
        return nz[there * steps + i // 2, (i % 2) * half : (i % 2 + 1) * half, :]

    def summed(there, carry):
        return carry + added(
            [omega[i, pl.ds(there, 1), :] * group_at(there, i) for i in range(long)]
        )

    carry_top = lax.fori_loop(chip + 1, chips, summed, jnp.zeros((half, modes), F32))
    carry_low = above[4, pl.ds(chip, 1), :] * carry_top + added(
        [above[5 + i, pl.ds(chip, 1), :] * group_at(chip, steps + i) for i in range(steps)]
    )
    kin_top = (above[2, pl.ds(chip, 1), :] * carry_top).astype(BF16)
    kin_low = (above[3, pl.ds(chip, 1), :] * carry_low).astype(BF16)
    slot = 2 * me_s + core

    out_low, out_top = kin.at[2 * ns], kin.at[2 * ns + 1]
    out_low[...] = kin_low
    out_top[...] = kin_top

    def low_to_plane(other):
        return pltpu.make_async_remote_copy(
            src_ref=out_low, dst_ref=kin.at[slot], send_sem=send.at[4], recv_sem=recv.at[4],
            device_id=(2 * chip, other), device_id_type=MESH,
        )

    def top_to_plane(other):
        return pltpu.make_async_remote_copy(
            src_ref=out_top, dst_ref=kin.at[slot], send_sem=send.at[4], recv_sem=recv.at[4],
            device_id=(2 * chip + 1, other), device_id_type=MESH,
        )

    all_copies(low_to_plane)
    all_copies(top_to_plane)

    @pl.when(core == 0)
    def _():
        top_to_plane(me_s).start()
        kin[slot] = kin_low

    @pl.when(core == 1)
    def _():
        low_to_plane(me_s).start()
        kin[slot] = kin_top

    noise_part(limits[3], total)

    wait_bytes(rows.at[0, pl.ds(0, ns - 1)], recv.at[2])
    loads[4].wait()
    halves = pltpu.make_async_remote_copy(
        src_ref=rows.at[core], dst_ref=rows.at[core], send_sem=send.at[6], recv_sem=recv.at[6],
        device_id=(sibling, me_s), device_id_type=MESH,
    )
    halves.start()

    wait_bytes(cs.at[pl.ds(0, (ns - 1) * long)], recv.at[1])
    wait_bytes(ps.at[pl.ds(0, ns - 1)], recv.at[3])
    c = [cs[pl.ds(i, ns, stride=long), :] for i in range(steps)]
    inv_s = cs[pl.ds(steps, ns, stride=long), :]
    pa, pb = ps[:, 0, :], ps[:, 1, :]
    now = pb + pa
    for i in range(steps):
        pa = pa * (c[i] * c[i])
        after = now + pa
        kept = now / after
        inner = kept * inv_s
        coef_s[i] = inner * lax.rsqrt(inner)
        if i < steps - 1:
            coef_a[i] = kept * c[i + 1]
        now = after

    halves.wait_recv()
    wait_bytes(kin.at[pl.ds(0, 2 * ns - 1)], recv.at[4])

    for b in range(ns):
        value = jnp.concatenate([kin[2 * b], kin[2 * b + 1]], axis=0).astype(F32)
        for i in range(steps - 1, -1, -1):
            if i < steps - 1:
                value = coef_a[i, pl.ds(b, 1), :] * value
            value = value + coef_s[i, pl.ds(b, 1), :] * nz[(chips + b) * steps + i]
            vals[b, pl.ds(i * vecs, vecs), :] = value.astype(BF16)
        product = lax.dot_general(
            jnp.concatenate([rows[0, b], rows[1, b]], axis=0), vals[b], (((1,), (1,)), ((), ())), preferred_element_type=F32
        )
        if b == 0:
            out_ref[...] = product
        else:
            out_ref[...] += product

    wait_bytes(cz.at[pl.ds(0, (chips - 1) * steps)], send.at[0])
    wait_bytes(cs.at[pl.ds(0, (ns - 1) * long)], send.at[1])
    wait_bytes(rows.at[0, pl.ds(0, ns - 1)], send.at[2])
    halves.wait_send()
    wait_bytes(ps.at[pl.ds(0, ns - 1)], send.at[3])
    wait_bytes(kin.at[pl.ds(0, 2 * ns - 1)], send.at[4])
    across.wait_send()


def solution(mesh):
    zt, ns = mesh.shape["tm"], mesh.shape["space"]

    def local(spectrum, coupling, spatial_basis, noise_keys, noise_counters):
        steps, modes = coupling.shape
        vecs = noise_keys.shape[0]
        nodes = spatial_basis.shape[0] // ns
        vmem, smem = pltpu.VMEM, pltpu.SMEM
        return pl.pallas_call(
            functools.partial(kernel, zt, ns, steps, vecs),
            out_shape=jax.ShapeDtypeStruct((nodes, steps * vecs), F32),
            in_specs=[pl.BlockSpec(memory_space=pltpu.HBM)] * 5,
            out_specs=pl.BlockSpec(memory_space=vmem),
            scratch_shapes=[
                smem((vecs,), I32),
                smem((vecs,), I32),
                vmem((1, modes), F32),
                vmem((steps, modes), F32),
                vmem((2, vecs, modes), I32),
                vmem((2 * steps, modes), F32),
                vmem((zt * steps, modes), F32),
                vmem((2 * steps * ns, modes), F32),
                vmem((ns, 2, modes), F32),
                vmem((2, ns, nodes // 2, modes), BF16),
                vmem((2 * ns + 2, vecs // 2, modes), BF16),
                vmem((2, modes), F32),
                vmem(((zt // 2 + ns) * steps, vecs, modes), F32),
                vmem((2 * steps, zt // 2, modes), F32),
                vmem((5 + steps, zt // 2, modes), F32),
                vmem((steps, ns, modes), F32),
                vmem((steps, ns, modes), F32),
                vmem((ns, steps * vecs, modes), BF16),
                pltpu.SemaphoreType.DMA((7,)),
                pltpu.SemaphoreType.DMA((7,)),
                pltpu.SemaphoreType.DMA((5,)),
                pltpu.SemaphoreType.REGULAR((5,)),
            ],
            compiler_params=pltpu.CompilerParams(
                collective_id=0, has_side_effects=True, vmem_limit_bytes=62 * 2**20
            ),
        )(noise_keys, noise_counters, spectrum.reshape(1, modes), coupling, spatial_basis)

    return jax.shard_map(
        local,
        mesh=mesh,
        in_specs=(P("space"), P("tm", "space"), P(None, "space"), P(), P()),
        out_specs=P("space", "tm"),
        check_vma=False,
    )
```

```python
import functools

import jax
import jax.numpy as jnp
from jax import lax
from jax.experimental import pallas as pl
from jax.experimental.pallas import tpu as pltpu
from jax.sharding import PartitionSpec as P

MESH = pl.DeviceIdType.MESH
F32, BF16, I32 = jnp.float32, jnp.bfloat16, jnp.int32
KEY_STEP, TIME_STEP, MODE_STEP = 668265261, 374761393, -1640531535
SINE = (
    6.283185160088995,
    -41.3416550313122,
    81.60100406725992,
    -76.54978216547879,
    39.536705154320686,
)


def mix_bits(h):
    h = h ^ lax.shift_right_logical(h, I32(16))
    h = h * I32(-2048144789)
    h = h ^ lax.shift_right_logical(h, I32(13))
    h = h * I32(-1028477387)
    return h ^ lax.shift_right_logical(h, I32(16))


def noise_of(h):
    first = mix_bits(h)
    second = mix_bits(first + I32(1013904223))
    unit = (lax.shift_right_logical(first, I32(8)).astype(F32) + 0.5) * (1.0 / 16777216.0)
    square = -2.0 * jnp.log(unit)
    radius = square * lax.rsqrt(jnp.maximum(square, 1e-30))
    turn = jnp.abs(lax.shift_right_arithmetic(second, I32(8)).astype(F32) + 0.5)
    y = 0.25 - turn * (1.0 / 16777216.0)
    y2 = y * y
    p = jnp.float32(SINE[-1])
    for c in SINE[-2::-1]:
        p = p * y2 + jnp.float32(c)
    return radius * (p * y)


def shifted(x, by, fill):
    return jnp.concatenate([jnp.full((by, x.shape[1]), fill, F32), x[:-by]], axis=0)


def kernel(
    zt, ns, steps, vecs,
    keys_hbm, counters_hbm, spec_hbm, coup_hbm, basis_ref, out_ref,
    keys_ref, counters_ref, spec_ref, coup_ref, base, fixed, cz, cs, ps, rows, kin, mine,
    nz, omega, above, coef_s, coef_a, vals,
    send, recv, local_sem, meet,
):
    modes = coup_ref.shape[1]
    nodes = basis_ref.shape[0] // ns
    half = vecs // 2
    chips, long = zt // 2, 2 * steps
    me_t, me_s = lax.axis_index("tm"), lax.axis_index("space")
    core = lax.rem(me_t, 2)
    sibling = me_t + 1 - 2 * core
    chip = me_t // 2

    split, outer = chips // 2, chips * 3 // 4
    leading = chip < split
    third = jnp.logical_and(chip >= split, chip < outer)
    is_hub = chip == split - 1
    line_in, near_in, plane_in, line_go, plane_go = (meet.at[k] for k in range(5))
    barrier = pltpu.get_barrier_semaphore()

    def signal(sem, t, s):
        pl.semaphore_signal(sem, inc=1, device_id=(t, s), device_id_type=MESH)

    def signal_plane(sem):
        signal(sem, sibling, me_s)

        @pl.loop(1, ns)
        def _(j):
            other = lax.rem(me_s + j, ns)
            signal(sem, me_t, other)
            signal(sem, sibling, other)

    @pl.when(leading)
    def _():
        @pl.loop(1, chips)
        def _(j):
            signal(barrier, lax.rem(me_t + 2 * j, zt), me_s)

    @pl.when(jnp.logical_not(third))
    def _():
        signal_plane(barrier)

    @pl.when(chip >= outer)
    def _():
        @pl.loop(outer, chips)
        def _(to):
            @pl.when(to != chip)
            def _():
                signal(barrier, 2 * to + core, me_s)

    def half_rows(owner):
        start = owner * nodes + core * (nodes // 2)
        return pl.ds(pl.multiple_of(start, nodes // 2), nodes // 2)

    loads = [
        pltpu.make_async_copy(src, dst, local_sem.at[k])
        for k, (src, dst) in enumerate(
            [
                (keys_hbm, keys_ref),
                (counters_hbm, counters_ref),
                (spec_hbm, spec_ref),
                (coup_hbm, coup_ref),
                (basis_ref.at[half_rows(me_s), :], rows.at[core, me_s]),
            ]
        )
    ]
    for load in loads:
        load.start()
    loads[0].wait()
    loads[1].wait()

    lanes = lax.broadcasted_iota(I32, (1, modes), 1) * I32(MODE_STEP)
    for v in range(vecs):
        seed = keys_ref[v] * I32(KEY_STEP) + counters_ref[v] * I32(TIME_STEP)
        base[0, pl.ds(v, 1), :] = lanes + seed

    halved = base[0, pl.ds(pl.multiple_of(core * half, half), half), :]
    base[1, 0:half, :] = halved
    base[1, half:vecs, :] = halved + I32(TIME_STEP)

    n_group = chips - chip
    total = n_group + ns
    limits = [
        jnp.where(leading, 19 - 2 * chip, jnp.maximum(0, chip - split - 3)),
        jnp.where(leading, 22 - 2 * chip, 13),
        jnp.where(leading, 28 - 2 * chip, 18),
        total,
    ]
    limits = [jnp.clip(limit, 0, total - ns // 2) for limit in limits]

    def noise_part(lo, hi):
        @pl.loop(lo, hi)
        def _(u):
            group = u < n_group
            there, block = chips - 1 - u, u - n_group
            start = jnp.where(group, there * long, me_t * steps)
            mode = jnp.where(group, me_s, block) * modes
            offset = mode * I32(MODE_STEP) + start * I32(TIME_STEP)
            stride = jnp.where(group, I32(2 * TIME_STEP), I32(TIME_STEP))
            at = jnp.where(group, there, chips + block) * steps
            kind = jnp.where(group, 1, 0)

            @pl.loop(0, steps)
            def _(i):
                nz[at + i] = noise_of(base[kind] + (offset + i * stride))

    noise_part(0, limits[0])

    def wait_bytes(ref, sem):
        pltpu.make_async_copy(ref, ref, sem).wait()

    def tile(index):
        return pl.ds(pl.multiple_of(index * steps, steps), steps)

    loads[3].wait()
    mine_at = core * chips + chip
    cz[tile(mine_at), :] = coup_ref[...]
    loads[2].wait()
    inverse_spec = 1.0 / spec_ref[...]
    fixed[0:steps, :] = coup_ref[...]
    fixed[steps : 2 * steps, :] = jnp.broadcast_to(inverse_spec, (steps, modes))
    own_fixed = pl.ds(pl.multiple_of(me_s * long, long), long)
    cs[own_fixed, :] = fixed[...]

    def to_chips(lo, hi, k=0):
        @pl.loop(lo, hi)
        def _(to):
            @pl.when(to != chip)
            def _():
                pltpu.make_async_remote_copy(
                    src_ref=coup_ref, dst_ref=cz.at[tile(mine_at)],
                    send_sem=send.at[0], recv_sem=recv.at[k],
                    device_id=(2 * to + core, me_s), device_id_type=MESH,
                ).start()

    def all_copies(make):
        @pl.loop(1, ns)
        def _(j):
            make(lax.rem(me_s + j, ns)).start()

    def coupling_to_plane(other):
        return pltpu.make_async_remote_copy(
            src_ref=fixed, dst_ref=cs.at[own_fixed], send_sem=send.at[1], recv_sem=recv.at[1],
            device_id=(me_t, other), device_id_type=MESH,
        )

    def basis_to_plane(other):
        return pltpu.make_async_remote_copy(
            src_ref=basis_ref.at[half_rows(other), :],
            dst_ref=rows.at[core, me_s], send_sem=send.at[2], recv_sem=recv.at[2],
            device_id=(me_t, other), device_id_type=MESH,
        )

    def passed_on(side):
        count = (outer - split) * steps
        return cz.at[pl.ds(pl.multiple_of((side * chips + split) * steps, steps), count)]

    def signal_chips(sem, lo, hi):
        @pl.loop(lo, hi)
        def _(to):
            signal(sem, 2 * to + core, me_s)

    @pl.when(leading)
    def _():
        pl.semaphore_wait(barrier, split - 1 + 1 + 2 * (ns - 1))
        to_chips(0, split)
        all_copies(coupling_to_plane)
        all_copies(basis_to_plane)

    @pl.when(jnp.logical_not(leading))
    def _():
        @pl.when(third)
        def _():
            pl.semaphore_wait(barrier, split)

        @pl.when(chip >= outer)
        def _():
            pl.semaphore_wait(barrier, split + chips - outer - 1 + 1 + 2 * (ns - 1))

        @pl.when(third)
        def _():
            to_chips(0, split, 7)
            signal(near_in, 2 * (split - 1) + core, me_s)

        signal_chips(line_in, 0, split)

        @pl.when(chip >= outer)
        def _():
            to_chips(0, split)
            to_chips(outer, chips)
            all_copies(coupling_to_plane)
            all_copies(basis_to_plane)

    noise_part(limits[0], limits[1])

    @pl.when(is_hub)
    def _():
        pl.semaphore_wait(near_in, outer - split)
        signal_plane(plane_in)

    @pl.when(third)
    def _():
        pl.semaphore_wait(plane_go, 1)
        to_chips(split, outer)
        all_copies(coupling_to_plane)
        all_copies(basis_to_plane)

    noise_part(limits[1], limits[2])

    @pl.when(is_hub)
    def _():
        pl.semaphore_wait(plane_in, 1 + 2 * (ns - 1))
        signal_chips(plane_go, split, outer)

    @pl.when(leading)
    def _():
        pl.semaphore_wait(line_in, chips - split)

        @pl.when(chip == 0)
        def _():
            signal_chips(line_go, outer, chips)

        to_chips(split, chips)
        wait_bytes(passed_on(0), recv.at[7])

    @pl.when(chip == 0)
    def _():
        @pl.loop(outer, chips)
        def _(to):
            pltpu.make_async_remote_copy(
                src_ref=passed_on(core), dst_ref=passed_on(core),
                send_sem=send.at[7], recv_sem=recv.at[0],
                device_id=(2 * to + core, me_s), device_id_type=MESH,
            ).start()

    @pl.when(chip >= outer)
    def _():
        pl.semaphore_wait(line_go, 1)
        to_chips(split, outer)

    noise_part(limits[2], limits[3])

    @pl.when(leading)
    def _():
        wait_bytes(cz.at[pl.ds(0, (chips - 1 - outer + split) * steps)], recv.at[0])

    @pl.when(jnp.logical_not(leading))
    def _():
        wait_bytes(cz.at[pl.ds(0, (chips - 1) * steps)], recv.at[0])

    line = pl.ds(pl.multiple_of(core * chips * steps, steps), chips * steps)
    across = pltpu.make_async_remote_copy(
        src_ref=cz.at[line], dst_ref=cz.at[line], send_sem=send.at[5], recv_sem=recv.at[5],
        device_id=(sibling, me_s), device_id_type=MESH,
    )
    across.start()
    across.wait_recv()

    c = [
        cz[pl.ds(p * chips * steps + i, chips, stride=steps), :]
        for p in range(2)
        for i in range(steps)
    ]
    one, nil = jnp.ones((chips, modes), F32), jnp.zeros((chips, modes), F32)
    alpha, beta = [one], [nil]
    for i in range(long + 1):
        beta.append(beta[i] + alpha[i])
        if i < long:
            alpha.append(alpha[i] * (c[i] * c[i]))
    pa, pb = alpha[long], beta[long]
    by = 1
    while by < chips:
        pb = shifted(pb, by, 0.0) + shifted(pa, by, 1.0) * pb
        pa = shifted(pa, by, 1.0) * pa
        by *= 2
    pa, pb = shifted(pa, 1, 1.0), shifted(pb, 1, 0.0)

    above[0] = jnp.where(core == 0, pa, pa * alpha[steps])
    above[1] = jnp.where(core == 0, pb, pb + pa * beta[steps])
    mine[0:1, :] = above[0, pl.ds(chip, 1), :]
    mine[1:2, :] = above[1, pl.ds(chip, 1), :]
    ps[me_s] = mine[...]

    def start_to_plane(other):
        return pltpu.make_async_remote_copy(
            src_ref=mine, dst_ref=ps.at[me_s], send_sem=send.at[3], recv_sem=recv.at[3],
            device_id=(me_t, other), device_id_type=MESH,
        )

    all_copies(start_to_plane)

    sums = [pb + pa * beta[i + 1] for i in range(long + 1)]
    inverse = [1.0 / sums[i + 1] for i in range(long)]
    keep = [sums[i] * inverse[i] for i in range(long)]
    gains, weight = [], []
    for first in (0, steps):
        gain = one
        for i in range(first, first + steps):
            inner = keep[i] * inverse_spec
            weight.append(gain * c[i] * (inner * lax.rsqrt(inner)))
            gain = gain * (c[i] * keep[i])
        gains.append(gain)
    numbers = lax.broadcasted_iota(I32, (chips, modes), 0)
    reach = jnp.where(numbers > chip, gains[0] * gains[1], 1.0)
    by = 1
    while by < chips:
        reach = shifted(reach, by, 1.0) * reach
        by *= 2
    reach = shifted(reach, 1, 1.0)
    middle = reach * gains[0]
    for i in range(steps):
        omega[i] = weight[i] * reach
        omega[steps + i] = weight[steps + i] * middle
        above[5 + i] = weight[steps + i]
    above[2] = keep[long - 1]
    above[3] = keep[steps - 1]
    above[4] = gains[1]

    def added(terms):
        while len(terms) > 1:
            terms = [terms[k] + terms[k + 1] for k in range(0, len(terms), 2)]
        return terms[0]

    def group_at(there, i):
        return nz[there * steps + i // 2, (i % 2) * half : (i % 2 + 1) * half, :]

    def summed(there, carry):
        return carry + added(
            [omega[i, pl.ds(there, 1), :] * group_at(there, i) for i in range(long)]
        )

    carry_top = lax.fori_loop(chip + 1, chips, summed, jnp.zeros((half, modes), F32))
    carry_low = above[4, pl.ds(chip, 1), :] * carry_top + added(
        [above[5 + i, pl.ds(chip, 1), :] * group_at(chip, steps + i) for i in range(steps)]
    )
    kin_top = (above[2, pl.ds(chip, 1), :] * carry_top).astype(BF16)
    kin_low = (above[3, pl.ds(chip, 1), :] * carry_low).astype(BF16)
    slot = 2 * me_s + core

    out_low, out_top = kin.at[2 * ns], kin.at[2 * ns + 1]
    out_low[...] = kin_low
    out_top[...] = kin_top

    def low_to_plane(other):
        return pltpu.make_async_remote_copy(
            src_ref=out_low, dst_ref=kin.at[slot], send_sem=send.at[4], recv_sem=recv.at[4],
            device_id=(2 * chip, other), device_id_type=MESH,
        )

    def top_to_plane(other):
        return pltpu.make_async_remote_copy(
            src_ref=out_top, dst_ref=kin.at[slot], send_sem=send.at[4], recv_sem=recv.at[4],
            device_id=(2 * chip + 1, other), device_id_type=MESH,
        )

    all_copies(low_to_plane)
    all_copies(top_to_plane)

    @pl.when(core == 0)
    def _():
        top_to_plane(me_s).start()
        kin[slot] = kin_low

    @pl.when(core == 1)
    def _():
        low_to_plane(me_s).start()
        kin[slot] = kin_top

    noise_part(limits[3], total)

    wait_bytes(rows.at[0, pl.ds(0, ns - 1)], recv.at[2])
    loads[4].wait()
    halves = pltpu.make_async_remote_copy(
        src_ref=rows.at[core], dst_ref=rows.at[core], send_sem=send.at[6], recv_sem=recv.at[6],
        device_id=(sibling, me_s), device_id_type=MESH,
    )
    halves.start()

    wait_bytes(cs.at[pl.ds(0, (ns - 1) * long)], recv.at[1])
    wait_bytes(ps.at[pl.ds(0, ns - 1)], recv.at[3])
    c = [cs[pl.ds(i, ns, stride=long), :] for i in range(steps)]
    inv_s = cs[pl.ds(steps, ns, stride=long), :]
    pa, pb = ps[:, 0, :], ps[:, 1, :]
    now = pb + pa
    for i in range(steps):
        pa = pa * (c[i] * c[i])
        after = now + pa
        kept = now / after
        inner = kept * inv_s
        coef_s[i] = inner * lax.rsqrt(inner)
        if i < steps - 1:
            coef_a[i] = kept * c[i + 1]
        now = after

    halves.wait_recv()
    wait_bytes(kin.at[pl.ds(0, 2 * ns - 1)], recv.at[4])

    for b in range(ns):
        value = jnp.concatenate([kin[2 * b], kin[2 * b + 1]], axis=0).astype(F32)
        for i in range(steps - 1, -1, -1):
            if i < steps - 1:
                value = coef_a[i, pl.ds(b, 1), :] * value
            value = value + coef_s[i, pl.ds(b, 1), :] * nz[(chips + b) * steps + i]
            vals[b, pl.ds(i * vecs, vecs), :] = value.astype(BF16)
        product = lax.dot_general(
            jnp.concatenate([rows[0, b], rows[1, b]], axis=0), vals[b], (((1,), (1,)), ((), ())), preferred_element_type=F32
        )
        if b == 0:
            out_ref[...] = product
        else:
            out_ref[...] += product

    @pl.when(third)
    def _():
        wait_bytes(cz.at[pl.ds(0, (outer - 1) * steps)], send.at[0])

    @pl.when(jnp.logical_not(third))
    def _():
        wait_bytes(cz.at[pl.ds(0, (chips - 1) * steps)], send.at[0])

    @pl.when(chip == 0)
    def _():
        wait_bytes(cz.at[pl.ds(0, (chips - outer) * (outer - split) * steps)], send.at[7])

    wait_bytes(cs.at[pl.ds(0, (ns - 1) * long)], send.at[1])
    wait_bytes(rows.at[0, pl.ds(0, ns - 1)], send.at[2])
    halves.wait_send()
    wait_bytes(ps.at[pl.ds(0, ns - 1)], send.at[3])
    wait_bytes(kin.at[pl.ds(0, 2 * ns - 1)], send.at[4])
    across.wait_send()


def solution(mesh):
    zt, ns = mesh.shape["tm"], mesh.shape["space"]

    def local(spectrum, coupling, spatial_basis, noise_keys, noise_counters):
        steps, modes = coupling.shape
        vecs = noise_keys.shape[0]
        nodes = spatial_basis.shape[0] // ns
        vmem, smem = pltpu.VMEM, pltpu.SMEM
        return pl.pallas_call(
            functools.partial(kernel, zt, ns, steps, vecs),
            out_shape=jax.ShapeDtypeStruct((nodes, steps * vecs), F32),
            in_specs=[pl.BlockSpec(memory_space=pltpu.HBM)] * 5,
            out_specs=pl.BlockSpec(memory_space=vmem),
            scratch_shapes=[
                smem((vecs,), I32),
                smem((vecs,), I32),
                vmem((1, modes), F32),
                vmem((steps, modes), F32),
                vmem((2, vecs, modes), I32),
                vmem((2 * steps, modes), F32),
                vmem((zt * steps, modes), F32),
                vmem((2 * steps * ns, modes), F32),
                vmem((ns, 2, modes), F32),
                vmem((2, ns, nodes // 2, modes), BF16),
                vmem((2 * ns + 2, vecs // 2, modes), BF16),
                vmem((2, modes), F32),
                vmem(((zt // 2 + ns) * steps, vecs, modes), F32),
                vmem((2 * steps, zt // 2, modes), F32),
                vmem((5 + steps, zt // 2, modes), F32),
                vmem((steps, ns, modes), F32),
                vmem((steps, ns, modes), F32),
                vmem((ns, steps * vecs, modes), BF16),
                pltpu.SemaphoreType.DMA((8,)),
                pltpu.SemaphoreType.DMA((8,)),
                pltpu.SemaphoreType.DMA((5,)),
                pltpu.SemaphoreType.REGULAR((5,)),
            ],
            compiler_params=pltpu.CompilerParams(
                collective_id=0, has_side_effects=True, vmem_limit_bytes=62 * 2**20
            ),
        )(noise_keys, noise_counters, spectrum.reshape(1, modes), coupling, spatial_basis)

    return jax.shard_map(
        local,
        mesh=mesh,
        in_specs=(P("space"), P("tm", "space"), P(None, "space"), P(), P()),
        out_specs=P("space", "tm"),
        check_vma=False,
    )
```

```python
import functools

import jax
import jax.numpy as jnp
from jax import lax
from jax.experimental import pallas as pl
from jax.experimental.pallas import tpu as pltpu
from jax.sharding import PartitionSpec as P

MESH = pl.DeviceIdType.MESH
F32, BF16, I32 = jnp.float32, jnp.bfloat16, jnp.int32
KEY_STEP, TIME_STEP, MODE_STEP = 668265261, 374761393, -1640531535
SINE = (
    6.283185160088995,
    -41.3416550313122,
    81.60100406725992,
    -76.54978216547879,
    39.536705154320686,
)


def mix_bits(h):
    h = h ^ lax.shift_right_logical(h, I32(16))
    h = h * I32(-2048144789)
    h = h ^ lax.shift_right_logical(h, I32(13))
    h = h * I32(-1028477387)
    return h ^ lax.shift_right_logical(h, I32(16))


def noise_of(h):
    first = mix_bits(h)
    second = mix_bits(first + I32(1013904223))
    unit = (lax.shift_right_logical(first, I32(8)).astype(F32) + 0.5) * (1.0 / 16777216.0)
    square = -2.0 * jnp.log(unit)
    radius = square * lax.rsqrt(jnp.maximum(square, 1e-30))
    turn = jnp.abs(lax.shift_right_arithmetic(second, I32(8)).astype(F32) + 0.5)
    y = 0.25 - turn * (1.0 / 16777216.0)
    y2 = y * y
    p = jnp.float32(SINE[-1])
    for c in SINE[-2::-1]:
        p = p * y2 + jnp.float32(c)
    return radius * (p * y)


def shifted(x, by, fill):
    return jnp.concatenate([jnp.full((by, x.shape[1]), fill, F32), x[:-by]], axis=0)


def kernel(
    zt, ns, steps, vecs,
    keys_hbm, counters_hbm, spec_hbm, coup_hbm, basis_ref, out_ref,
    keys_ref, counters_ref, spec_ref, coup_ref, base, fixed, cz, cs, ps, rows, kin, mine,
    nz, omega, above, coef_s, coef_a, vals,
    send, recv, local_sem, meet, arrived,
):
    modes = coup_ref.shape[1]
    nodes = basis_ref.shape[0] // ns
    half = vecs // 2
    chips, long = zt // 2, 2 * steps
    me_t, me_s = lax.axis_index("tm"), lax.axis_index("space")
    core = lax.rem(me_t, 2)
    sibling = me_t + 1 - 2 * core
    chip = me_t // 2

    split, outer = chips // 2, chips * 3 // 4
    leading = chip < split
    third = jnp.logical_and(chip >= split, chip < outer)
    is_hub = chip == split - 1
    line_in, near_in, plane_in, line_go, plane_go = (meet.at[k] for k in range(5))
    barrier = pltpu.get_barrier_semaphore()

    side = 4 if ns == 16 else 1
    wide = ns // side
    offsets = sorted(
        ((dx, dy) for dx in range(side) for dy in range(wide) if dx or dy),
        key=lambda d: -min(d[0], side - d[0]) - min(d[1], wide - d[1]),
    )

    def partner(d):
        x, y = me_s // wide, lax.rem(me_s, wide)
        return lax.rem(x + d[0], side) * wide + lax.rem(y + d[1], wide)

    def signal(sem, t, s):
        pl.semaphore_signal(sem, inc=1, device_id=(t, s), device_id_type=MESH)

    def signal_plane(sem):
        signal(sem, sibling, me_s)

        @pl.loop(1, ns)
        def _(j):
            other = lax.rem(me_s + j, ns)
            signal(sem, me_t, other)
            signal(sem, sibling, other)

    @pl.when(leading)
    def _():
        @pl.loop(1, chips)
        def _(j):
            signal(barrier, lax.rem(me_t + 2 * j, zt), me_s)

    @pl.when(jnp.logical_not(third))
    def _():
        signal_plane(barrier)

    @pl.when(chip >= outer)
    def _():
        @pl.loop(outer, chips)
        def _(to):
            @pl.when(to != chip)
            def _():
                signal(barrier, 2 * to + core, me_s)

    def half_rows(owner):
        start = owner * nodes + core * (nodes // 2)
        return pl.ds(pl.multiple_of(start, nodes // 2), nodes // 2)

    loads = [
        pltpu.make_async_copy(src, dst, local_sem.at[k])
        for k, (src, dst) in enumerate(
            [
                (keys_hbm, keys_ref),
                (counters_hbm, counters_ref),
                (spec_hbm, spec_ref),
                (coup_hbm, coup_ref),
                (basis_ref.at[half_rows(me_s), :], rows.at[core, me_s]),
            ]
        )
    ]
    for load in loads:
        load.start()
    loads[0].wait()
    loads[1].wait()

    lanes = lax.broadcasted_iota(I32, (1, modes), 1) * I32(MODE_STEP)
    for v in range(vecs):
        seed = keys_ref[v] * I32(KEY_STEP) + counters_ref[v] * I32(TIME_STEP)
        base[0, pl.ds(v, 1), :] = lanes + seed

    halved = base[0, pl.ds(pl.multiple_of(core * half, half), half), :]
    base[1, 0:half, :] = halved
    base[1, half:vecs, :] = halved + I32(TIME_STEP)

    n_group = chips - chip
    total = n_group + ns
    limits = [
        jnp.where(leading, 19 - 2 * chip, jnp.maximum(0, chip - split - 3)),
        jnp.where(leading, 22 - 2 * chip, 13),
        jnp.where(leading, 28 - 2 * chip, 18),
        total,
    ]
    limits = [jnp.clip(limit, 0, total - ns // 2) for limit in limits]

    def noise_part(lo, hi):
        @pl.loop(lo, hi)
        def _(u):
            group = u < n_group
            there, block = chips - 1 - u, u - n_group
            start = jnp.where(group, there * long, me_t * steps)
            mode = jnp.where(group, me_s, block) * modes
            offset = mode * I32(MODE_STEP) + start * I32(TIME_STEP)
            stride = jnp.where(group, I32(2 * TIME_STEP), I32(TIME_STEP))
            at = jnp.where(group, there, chips + block) * steps
            kind = jnp.where(group, 1, 0)

            @pl.loop(0, steps)
            def _(i):
                nz[at + i] = noise_of(base[kind] + (offset + i * stride))

    noise_part(0, limits[0])

    def wait_bytes(ref, sem):
        pltpu.make_async_copy(ref, ref, sem).wait()

    def tile(index):
        return pl.ds(pl.multiple_of(index * steps, steps), steps)

    loads[3].wait()
    mine_at = core * chips + chip
    cz[tile(mine_at), :] = coup_ref[...]
    loads[2].wait()
    inverse_spec = 1.0 / spec_ref[...]
    fixed[0:steps, :] = coup_ref[...]
    fixed[steps : 2 * steps, :] = jnp.broadcast_to(inverse_spec, (steps, modes))
    own_fixed = pl.ds(pl.multiple_of(me_s * long, long), long)
    cs[own_fixed, :] = fixed[...]

    def to_chips(lo, hi, k=0):
        @pl.loop(lo, hi)
        def _(to):
            @pl.when(to != chip)
            def _():
                pltpu.make_async_remote_copy(
                    src_ref=coup_ref, dst_ref=cz.at[tile(mine_at)],
                    send_sem=send.at[0], recv_sem=recv.at[k],
                    device_id=(2 * to + core, me_s), device_id_type=MESH,
                ).start()

    def all_copies(make):
        @pl.loop(1, ns)
        def _(j):
            make(lax.rem(me_s + j, ns)).start()

    def coupling_to_plane(other):
        return pltpu.make_async_remote_copy(
            src_ref=fixed, dst_ref=cs.at[own_fixed], send_sem=send.at[1], recv_sem=recv.at[1],
            device_id=(me_t, other), device_id_type=MESH,
        )

    def basis_to_plane(other):
        return pltpu.make_async_remote_copy(
            src_ref=basis_ref.at[half_rows(other), :],
            dst_ref=rows.at[core, me_s], send_sem=send.at[2], recv_sem=recv.at[2],
            device_id=(me_t, other), device_id_type=MESH,
        )

    def passed_on(side):
        count = (outer - split) * steps
        return cz.at[pl.ds(pl.multiple_of((side * chips + split) * steps, steps), count)]

    def signal_chips(sem, lo, hi):
        @pl.loop(lo, hi)
        def _(to):
            signal(sem, 2 * to + core, me_s)

    @pl.when(leading)
    def _():
        pl.semaphore_wait(barrier, split - 1 + 1 + 2 * (ns - 1))
        to_chips(0, split)
        all_copies(coupling_to_plane)
        all_copies(basis_to_plane)

    @pl.when(jnp.logical_not(leading))
    def _():
        @pl.when(third)
        def _():
            pl.semaphore_wait(barrier, split)

        @pl.when(chip >= outer)
        def _():
            pl.semaphore_wait(barrier, split + chips - outer - 1 + 1 + 2 * (ns - 1))

        @pl.when(third)
        def _():
            to_chips(0, split, 7)
            signal(near_in, 2 * (split - 1) + core, me_s)

        signal_chips(line_in, 0, split)

        @pl.when(chip >= outer)
        def _():
            to_chips(0, split)
            to_chips(outer, chips)
            all_copies(coupling_to_plane)
            all_copies(basis_to_plane)

    noise_part(limits[0], limits[1])

    @pl.when(is_hub)
    def _():
        pl.semaphore_wait(near_in, outer - split)
        signal_plane(plane_in)

    @pl.when(third)
    def _():
        pl.semaphore_wait(plane_go, 1)
        to_chips(split, outer)
        all_copies(coupling_to_plane)
        all_copies(basis_to_plane)

    noise_part(limits[1], limits[2])

    @pl.when(is_hub)
    def _():
        pl.semaphore_wait(plane_in, 1 + 2 * (ns - 1))
        signal_chips(plane_go, split, outer)

    @pl.when(leading)
    def _():
        pl.semaphore_wait(line_in, chips - split)

        @pl.when(chip == 0)
        def _():
            signal_chips(line_go, outer, chips)

        to_chips(split, chips)
        wait_bytes(passed_on(0), recv.at[7])

    @pl.when(chip == 0)
    def _():
        @pl.loop(outer, chips)
        def _(to):
            pltpu.make_async_remote_copy(
                src_ref=passed_on(core), dst_ref=passed_on(core),
                send_sem=send.at[7], recv_sem=recv.at[0],
                device_id=(2 * to + core, me_s), device_id_type=MESH,
            ).start()

    @pl.when(chip >= outer)
    def _():
        pl.semaphore_wait(line_go, 1)
        to_chips(split, outer)

    noise_part(limits[2], limits[3])

    @pl.when(leading)
    def _():
        wait_bytes(cz.at[pl.ds(0, (chips - 1 - outer + split) * steps)], recv.at[0])

    @pl.when(jnp.logical_not(leading))
    def _():
        wait_bytes(cz.at[pl.ds(0, (chips - 1) * steps)], recv.at[0])

    line = pl.ds(pl.multiple_of(core * chips * steps, steps), chips * steps)
    across = pltpu.make_async_remote_copy(
        src_ref=cz.at[line], dst_ref=cz.at[line], send_sem=send.at[5], recv_sem=recv.at[5],
        device_id=(sibling, me_s), device_id_type=MESH,
    )
    across.start()
    across.wait_recv()

    c = [
        cz[pl.ds(p * chips * steps + i, chips, stride=steps), :]
        for p in range(2)
        for i in range(steps)
    ]
    one, nil = jnp.ones((chips, modes), F32), jnp.zeros((chips, modes), F32)
    alpha, beta = [one], [nil]
    for i in range(long + 1):
        beta.append(beta[i] + alpha[i])
        if i < long:
            alpha.append(alpha[i] * (c[i] * c[i]))
    pa, pb = alpha[long], beta[long]
    by = 1
    while by < chips:
        pb = shifted(pb, by, 0.0) + shifted(pa, by, 1.0) * pb
        pa = shifted(pa, by, 1.0) * pa
        by *= 2
    pa, pb = shifted(pa, 1, 1.0), shifted(pb, 1, 0.0)

    above[0] = jnp.where(core == 0, pa, pa * alpha[steps])
    above[1] = jnp.where(core == 0, pb, pb + pa * beta[steps])
    mine[0:1, :] = above[0, pl.ds(chip, 1), :]
    mine[1:2, :] = above[1, pl.ds(chip, 1), :]
    ps[me_s] = mine[...]

    def start_to_plane(other):
        return pltpu.make_async_remote_copy(
            src_ref=mine, dst_ref=ps.at[me_s], send_sem=send.at[3], recv_sem=recv.at[3],
            device_id=(me_t, other), device_id_type=MESH,
        )

    all_copies(start_to_plane)

    sums = [pb + pa * beta[i + 1] for i in range(long + 1)]
    inverse = [1.0 / sums[i + 1] for i in range(long)]
    keep = [sums[i] * inverse[i] for i in range(long)]
    gains, weight = [], []
    for first in (0, steps):
        gain = one
        for i in range(first, first + steps):
            inner = keep[i] * inverse_spec
            weight.append(gain * c[i] * (inner * lax.rsqrt(inner)))
            gain = gain * (c[i] * keep[i])
        gains.append(gain)
    numbers = lax.broadcasted_iota(I32, (chips, modes), 0)
    reach = jnp.where(numbers > chip, gains[0] * gains[1], 1.0)
    by = 1
    while by < chips:
        reach = shifted(reach, by, 1.0) * reach
        by *= 2
    reach = shifted(reach, 1, 1.0)
    middle = reach * gains[0]
    for i in range(steps):
        omega[i] = weight[i] * reach
        omega[steps + i] = weight[steps + i] * middle
        above[5 + i] = weight[steps + i]
    above[2] = keep[long - 1]
    above[3] = keep[steps - 1]
    above[4] = gains[1]

    def added(terms):
        while len(terms) > 1:
            terms = [terms[k] + terms[k + 1] for k in range(0, len(terms), 2)]
        return terms[0]

    def group_at(there, i):
        return nz[there * steps + i // 2, (i % 2) * half : (i % 2 + 1) * half, :]

    def summed(there, carry):
        return carry + added(
            [omega[i, pl.ds(there, 1), :] * group_at(there, i) for i in range(long)]
        )

    carry_top = lax.fori_loop(chip + 1, chips, summed, jnp.zeros((half, modes), F32))
    kin_top = (above[2, pl.ds(chip, 1), :] * carry_top).astype(BF16)
    slot = 2 * me_s + core

    out_low, out_top = kin.at[2 * ns], kin.at[2 * ns + 1]
    out_top[...] = kin_top

    def to_plane(source, t, other):
        return pltpu.make_async_remote_copy(
            src_ref=source, dst_ref=kin.at[slot], send_sem=send.at[4], recv_sem=arrived.at[me_s],
            device_id=(t, other), device_id_type=MESH,
        )

    @pl.when(chip == 0)
    def _():
        for d in offsets:
            to_plane(out_top, 2 * chip + 1, partner(d)).start()

    carry_low = above[4, pl.ds(chip, 1), :] * carry_top + added(
        [above[5 + i, pl.ds(chip, 1), :] * group_at(chip, steps + i) for i in range(steps)]
    )
    kin_low = (above[3, pl.ds(chip, 1), :] * carry_low).astype(BF16)
    out_low[...] = kin_low

    @pl.when(chip == 0)
    def _():
        for d in offsets:
            to_plane(out_low, 2 * chip, partner(d)).start()

    @pl.when(chip > 0)
    def _():
        for d in offsets:
            to_plane(out_top, 2 * chip + 1, partner(d)).start()
            to_plane(out_low, 2 * chip, partner(d)).start()

    @pl.when(core == 0)
    def _():
        to_plane(out_top, sibling, me_s).start()
        kin[slot] = kin_low

    @pl.when(core == 1)
    def _():
        to_plane(out_low, sibling, me_s).start()
        kin[slot] = kin_top

    noise_part(limits[3], total)

    wait_bytes(rows.at[0, pl.ds(0, ns - 1)], recv.at[2])
    loads[4].wait()
    halves = pltpu.make_async_remote_copy(
        src_ref=rows.at[core], dst_ref=rows.at[core], send_sem=send.at[6], recv_sem=recv.at[6],
        device_id=(sibling, me_s), device_id_type=MESH,
    )
    halves.start()

    wait_bytes(cs.at[pl.ds(0, (ns - 1) * long)], recv.at[1])
    wait_bytes(ps.at[pl.ds(0, ns - 1)], recv.at[3])
    c = [cs[pl.ds(i, ns, stride=long), :] for i in range(steps)]
    inv_s = cs[pl.ds(steps, ns, stride=long), :]
    pa, pb = ps[:, 0, :], ps[:, 1, :]
    now = pb + pa
    for i in range(steps):
        pa = pa * (c[i] * c[i])
        after = now + pa
        kept = now / after
        inner = kept * inv_s
        coef_s[i] = inner * lax.rsqrt(inner)
        if i < steps - 1:
            coef_a[i] = kept * c[i + 1]
        now = after

    halves.wait_recv()

    order = [(0, 0), *offsets]
    blocks = [partner(d) if k else me_s for k, d in enumerate(order)]
    stops = [ns * g // 2 for g in range(2 + 1)]
    for k, b in enumerate(blocks):
        if k in stops:
            for q in range(k, stops[stops.index(k) + 1]):
                wait_bytes(kin.at[pl.ds(0, 2 if q else 1)], arrived.at[blocks[q]])
        value = jnp.concatenate([kin[2 * b], kin[2 * b + 1]], axis=0).astype(F32)
        for i in range(steps - 1, -1, -1):
            if i < steps - 1:
                value = coef_a[i, pl.ds(b, 1), :] * value
            value = value + coef_s[i, pl.ds(b, 1), :] * nz[(chips + b) * steps + i]
            vals[b, pl.ds(i * vecs, vecs), :] = value.astype(BF16)
        product = lax.dot_general(
            jnp.concatenate([rows[0, b], rows[1, b]], axis=0), vals[b], (((1,), (1,)), ((), ())), preferred_element_type=F32
        )
        if k == 0:
            out_ref[...] = product
        else:
            out_ref[...] += product

    @pl.when(third)
    def _():
        wait_bytes(cz.at[pl.ds(0, (outer - 1) * steps)], send.at[0])

    @pl.when(jnp.logical_not(third))
    def _():
        wait_bytes(cz.at[pl.ds(0, (chips - 1) * steps)], send.at[0])

    @pl.when(chip == 0)
    def _():
        wait_bytes(cz.at[pl.ds(0, (chips - outer) * (outer - split) * steps)], send.at[7])

    wait_bytes(cs.at[pl.ds(0, (ns - 1) * long)], send.at[1])
    wait_bytes(rows.at[0, pl.ds(0, ns - 1)], send.at[2])
    halves.wait_send()
    wait_bytes(ps.at[pl.ds(0, ns - 1)], send.at[3])
    wait_bytes(kin.at[pl.ds(0, 2 * ns - 1)], send.at[4])
    across.wait_send()


def solution(mesh):
    zt, ns = mesh.shape["tm"], mesh.shape["space"]

    def local(spectrum, coupling, spatial_basis, noise_keys, noise_counters):
        steps, modes = coupling.shape
        vecs = noise_keys.shape[0]
        nodes = spatial_basis.shape[0] // ns
        vmem, smem = pltpu.VMEM, pltpu.SMEM
        return pl.pallas_call(
            functools.partial(kernel, zt, ns, steps, vecs),
            out_shape=jax.ShapeDtypeStruct((nodes, steps * vecs), F32),
            in_specs=[pl.BlockSpec(memory_space=pltpu.HBM)] * 5,
            out_specs=pl.BlockSpec(memory_space=vmem),
            scratch_shapes=[
                smem((vecs,), I32),
                smem((vecs,), I32),
                vmem((1, modes), F32),
                vmem((steps, modes), F32),
                vmem((2, vecs, modes), I32),
                vmem((2 * steps, modes), F32),
                vmem((zt * steps, modes), F32),
                vmem((2 * steps * ns, modes), F32),
                vmem((ns, 2, modes), F32),
                vmem((2, ns, nodes // 2, modes), BF16),
                vmem((2 * ns + 2, vecs // 2, modes), BF16),
                vmem((2, modes), F32),
                vmem(((zt // 2 + ns) * steps, vecs, modes), F32),
                vmem((2 * steps, zt // 2, modes), F32),
                vmem((5 + steps, zt // 2, modes), F32),
                vmem((steps, ns, modes), F32),
                vmem((steps, ns, modes), F32),
                vmem((ns, steps * vecs, modes), BF16),
                pltpu.SemaphoreType.DMA((8,)),
                pltpu.SemaphoreType.DMA((8,)),
                pltpu.SemaphoreType.DMA((5,)),
                pltpu.SemaphoreType.REGULAR((5,)),
                pltpu.SemaphoreType.DMA((ns,)),
            ],
            compiler_params=pltpu.CompilerParams(
                collective_id=0, has_side_effects=True, vmem_limit_bytes=62 * 2**20
            ),
        )(noise_keys, noise_counters, spectrum.reshape(1, modes), coupling, spatial_basis)

    return jax.shard_map(
        local,
        mesh=mesh,
        in_specs=(P("space"), P("tm", "space"), P(None, "space"), P(), P()),
        out_specs=P("space", "tm"),
        check_vma=False,
    )
```

```python
import functools

import jax
import jax.numpy as jnp
from jax import lax
from jax.experimental import pallas as pl
from jax.experimental.pallas import tpu as pltpu
from jax.sharding import PartitionSpec as P

MESH = pl.DeviceIdType.MESH
F32, BF16, I32 = jnp.float32, jnp.bfloat16, jnp.int32
KEY_STEP, TIME_STEP, MODE_STEP = 668265261, 374761393, -1640531535
SINE = (
    6.283185160088995,
    -41.3416550313122,
    81.60100406725992,
    -76.54978216547879,
    39.536705154320686,
)


def mix_bits(h):
    h = h ^ lax.shift_right_logical(h, I32(16))
    h = h * I32(-2048144789)
    h = h ^ lax.shift_right_logical(h, I32(13))
    h = h * I32(-1028477387)
    return h ^ lax.shift_right_logical(h, I32(16))


def noise_of(h):
    first = mix_bits(h)
    second = mix_bits(first + I32(1013904223))
    unit = (lax.shift_right_logical(first, I32(8)).astype(F32) + 0.5) * (1.0 / 16777216.0)
    square = -2.0 * jnp.log(unit)
    radius = square * lax.rsqrt(jnp.maximum(square, 1e-30))
    turn = jnp.abs(lax.shift_right_arithmetic(second, I32(8)).astype(F32) + 0.5)
    y = 0.25 - turn * (1.0 / 16777216.0)
    y2 = y * y
    p = jnp.float32(SINE[-1])
    for c in SINE[-2::-1]:
        p = p * y2 + jnp.float32(c)
    return radius * (p * y)


def shifted(x, by, fill):
    return jnp.concatenate([jnp.full((by, x.shape[1]), fill, F32), x[:-by]], axis=0)


def kernel(
    zt, ns, steps, vecs,
    keys_hbm, counters_hbm, spec_hbm, coup_hbm, basis_ref, out_ref,
    keys_ref, counters_ref, spec_ref, coup_ref, base, fixed, cz, cs, ps, rows, kin, mine,
    nz, omega, above, coef_s, coef_a, vals,
    send, recv, local_sem, meet,
):
    modes = coup_ref.shape[1]
    nodes = basis_ref.shape[0] // ns
    half = vecs // 2
    chips, long = zt // 2, 2 * steps
    me_t, me_s = lax.axis_index("tm"), lax.axis_index("space")
    core = lax.rem(me_t, 2)
    sibling = me_t + 1 - 2 * core
    chip = me_t // 2

    split, outer = chips // 2, chips * 3 // 4
    leading = chip < split
    third = jnp.logical_and(chip >= split, chip < outer)
    is_hub = chip == split - 1
    line_in, near_in, plane_in, line_go, plane_go = (meet.at[k] for k in range(5))
    barrier = pltpu.get_barrier_semaphore()

    def signal(sem, t, s):
        pl.semaphore_signal(sem, inc=1, device_id=(t, s), device_id_type=MESH)

    def signal_plane(sem):
        signal(sem, sibling, me_s)

        @pl.loop(1, ns)
        def _(j):
            other = lax.rem(me_s + j, ns)
            signal(sem, me_t, other)
            signal(sem, sibling, other)

    @pl.when(leading)
    def _():
        @pl.loop(1, chips)
        def _(j):
            signal(barrier, lax.rem(me_t + 2 * j, zt), me_s)

    @pl.when(jnp.logical_not(third))
    def _():
        signal_plane(barrier)

    @pl.when(chip >= outer)
    def _():
        @pl.loop(outer, chips)
        def _(to):
            @pl.when(to != chip)
            def _():
                signal(barrier, 2 * to + core, me_s)

    def half_rows(owner):
        start = owner * nodes + core * (nodes // 2)
        return pl.ds(pl.multiple_of(start, nodes // 2), nodes // 2)

    loads = [
        pltpu.make_async_copy(src, dst, local_sem.at[k])
        for k, (src, dst) in enumerate(
            [
                (keys_hbm, keys_ref),
                (counters_hbm, counters_ref),
                (spec_hbm, spec_ref),
                (coup_hbm, coup_ref),
                (basis_ref.at[half_rows(me_s), :], rows.at[core, me_s]),
            ]
        )
    ]
    for load in loads:
        load.start()
    loads[0].wait()
    loads[1].wait()

    lanes = lax.broadcasted_iota(I32, (1, modes), 1) * I32(MODE_STEP)
    for v in range(vecs):
        seed = keys_ref[v] * I32(KEY_STEP) + counters_ref[v] * I32(TIME_STEP)
        base[0, pl.ds(v, 1), :] = lanes + seed

    halved = base[0, pl.ds(pl.multiple_of(core * half, half), half), :]
    base[1, 0:half, :] = halved
    base[1, half:vecs, :] = halved + I32(TIME_STEP)

    n_group = chips - chip
    total = n_group + ns
    limits = [
        jnp.where(leading, 19 - 2 * chip, jnp.maximum(0, chip - split - 3)),
        jnp.where(leading, 22 - 2 * chip, 13),
        jnp.where(leading, 28 - 2 * chip, 18),
        total,
    ]
    limits = [jnp.clip(limit, 0, total - ns // 2) for limit in limits]

    def noise_part(lo, hi):
        @pl.loop(lo, hi)
        def _(u):
            group = u < n_group
            there, block = chips - 1 - u, u - n_group
            start = jnp.where(group, there * long, me_t * steps)
            mode = jnp.where(group, me_s, block) * modes
            offset = mode * I32(MODE_STEP) + start * I32(TIME_STEP)
            stride = jnp.where(group, I32(2 * TIME_STEP), I32(TIME_STEP))
            at = jnp.where(group, there, chips + block) * steps
            kind = jnp.where(group, 1, 0)

            @pl.loop(0, steps)
            def _(i):
                nz[at + i] = noise_of(base[kind] + (offset + i * stride))

    noise_part(0, limits[0])

    def wait_bytes(ref, sem):
        pltpu.make_async_copy(ref, ref, sem).wait()

    def tile(index):
        return pl.ds(pl.multiple_of(index * steps, steps), steps)

    loads[3].wait()
    mine_at = core * chips + chip
    cz[tile(mine_at), :] = coup_ref[...]
    loads[2].wait()
    inverse_spec = 1.0 / spec_ref[...]
    fixed[0:steps, :] = coup_ref[...]
    fixed[steps : 2 * steps, :] = jnp.broadcast_to(inverse_spec, (steps, modes))
    own_fixed = pl.ds(pl.multiple_of(me_s * long, long), long)
    cs[own_fixed, :] = fixed[...]

    def to_chips(lo, hi, k=0):
        @pl.loop(lo, hi)
        def _(to):
            @pl.when(to != chip)
            def _():
                pltpu.make_async_remote_copy(
                    src_ref=coup_ref, dst_ref=cz.at[tile(mine_at)],
                    send_sem=send.at[0], recv_sem=recv.at[k],
                    device_id=(2 * to + core, me_s), device_id_type=MESH,
                ).start()

    def all_copies(make):
        @pl.loop(1, ns)
        def _(j):
            make(lax.rem(me_s + j, ns)).start()

    def coupling_to_plane(other):
        return pltpu.make_async_remote_copy(
            src_ref=fixed, dst_ref=cs.at[own_fixed], send_sem=send.at[1], recv_sem=recv.at[1],
            device_id=(me_t, other), device_id_type=MESH,
        )

    def basis_to_plane(other):
        return pltpu.make_async_remote_copy(
            src_ref=basis_ref.at[half_rows(other), :],
            dst_ref=rows.at[core, me_s], send_sem=send.at[2], recv_sem=recv.at[2],
            device_id=(me_t, other), device_id_type=MESH,
        )

    def passed_on(side):
        count = (outer - split) * steps
        return cz.at[pl.ds(pl.multiple_of((side * chips + split) * steps, steps), count)]

    def signal_chips(sem, lo, hi):
        @pl.loop(lo, hi)
        def _(to):
            signal(sem, 2 * to + core, me_s)

    @pl.when(leading)
    def _():
        pl.semaphore_wait(barrier, split - 1 + 1 + 2 * (ns - 1))
        to_chips(0, split)
        all_copies(coupling_to_plane)
        all_copies(basis_to_plane)

    @pl.when(jnp.logical_not(leading))
    def _():
        @pl.when(third)
        def _():
            pl.semaphore_wait(barrier, split)

        @pl.when(chip >= outer)
        def _():
            pl.semaphore_wait(barrier, split + chips - outer - 1 + 1 + 2 * (ns - 1))

        @pl.when(third)
        def _():
            to_chips(0, split, 7)
            signal(near_in, 2 * (split - 1) + core, me_s)

        signal_chips(line_in, 0, split)

        @pl.when(chip >= outer)
        def _():
            to_chips(0, split)
            to_chips(outer, chips)
            all_copies(coupling_to_plane)
            all_copies(basis_to_plane)

    noise_part(limits[0], limits[1])

    @pl.when(is_hub)
    def _():
        pl.semaphore_wait(near_in, outer - split)
        signal_plane(plane_in)

    @pl.when(third)
    def _():
        pl.semaphore_wait(plane_go, 1)
        to_chips(split, outer)
        all_copies(coupling_to_plane)
        all_copies(basis_to_plane)

    noise_part(limits[1], limits[2])

    @pl.when(is_hub)
    def _():
        pl.semaphore_wait(plane_in, 1 + 2 * (ns - 1))
        signal_chips(plane_go, split, outer)

    @pl.when(leading)
    def _():
        pl.semaphore_wait(line_in, chips - split)

        @pl.when(chip == 0)
        def _():
            signal_chips(line_go, outer, chips)

        to_chips(split, chips)
        wait_bytes(passed_on(0), recv.at[7])

    @pl.when(chip == 0)
    def _():
        @pl.loop(outer, chips)
        def _(to):
            pltpu.make_async_remote_copy(
                src_ref=passed_on(core), dst_ref=passed_on(core),
                send_sem=send.at[7], recv_sem=recv.at[0],
                device_id=(2 * to + core, me_s), device_id_type=MESH,
            ).start()

    @pl.when(chip >= outer)
    def _():
        pl.semaphore_wait(line_go, 1)
        to_chips(split, outer)

    noise_part(limits[2], limits[3])

    @pl.when(leading)
    def _():
        wait_bytes(cz.at[pl.ds(0, (chips - 1 - outer + split) * steps)], recv.at[0])

    @pl.when(jnp.logical_not(leading))
    def _():
        wait_bytes(cz.at[pl.ds(0, (chips - 1) * steps)], recv.at[0])

    line = pl.ds(pl.multiple_of(core * chips * steps, steps), chips * steps)
    across = pltpu.make_async_remote_copy(
        src_ref=cz.at[line], dst_ref=cz.at[line], send_sem=send.at[5], recv_sem=recv.at[5],
        device_id=(sibling, me_s), device_id_type=MESH,
    )
    across.start()
    across.wait_recv()

    c = [
        cz[pl.ds(p * chips * steps + i, chips, stride=steps), :]
        for p in range(2)
        for i in range(steps)
    ]
    one, nil = jnp.ones((chips, modes), F32), jnp.zeros((chips, modes), F32)
    alpha, beta = [one], [nil]
    for i in range(long + 1):
        beta.append(beta[i] + alpha[i])
        if i < long:
            alpha.append(alpha[i] * (c[i] * c[i]))
    pa, pb = alpha[long], beta[long]
    by = 1
    while by < chips:
        pb = shifted(pb, by, 0.0) + shifted(pa, by, 1.0) * pb
        pa = shifted(pa, by, 1.0) * pa
        by *= 2
    pa, pb = shifted(pa, 1, 1.0), shifted(pb, 1, 0.0)

    above[0] = jnp.where(core == 0, pa, pa * alpha[steps])
    above[1] = jnp.where(core == 0, pb, pb + pa * beta[steps])
    mine[0:1, :] = above[0, pl.ds(chip, 1), :]
    mine[1:2, :] = above[1, pl.ds(chip, 1), :]
    ps[me_s] = mine[...]

    def start_to_plane(other):
        return pltpu.make_async_remote_copy(
            src_ref=mine, dst_ref=ps.at[me_s], send_sem=send.at[3], recv_sem=recv.at[3],
            device_id=(me_t, other), device_id_type=MESH,
        )

    all_copies(start_to_plane)

    sums = [pb + pa * beta[i + 1] for i in range(long + 1)]
    inverse = [1.0 / sums[i + 1] for i in range(long)]
    keep = [sums[i] * inverse[i] for i in range(long)]
    gains, weight = [], []
    for first in (0, steps):
        gain = one
        for i in range(first, first + steps):
            inner = keep[i] * inverse_spec
            weight.append(gain * c[i] * (inner * lax.rsqrt(inner)))
            gain = gain * (c[i] * keep[i])
        gains.append(gain)
    numbers = lax.broadcasted_iota(I32, (chips, modes), 0)
    reach = jnp.where(numbers > chip, gains[0] * gains[1], 1.0)
    by = 1
    while by < chips:
        reach = shifted(reach, by, 1.0) * reach
        by *= 2
    reach = shifted(reach, 1, 1.0)
    middle = reach * gains[0]
    for i in range(steps):
        omega[i] = weight[i] * reach
        omega[steps + i] = weight[steps + i] * middle
        above[5 + i] = weight[steps + i]
    above[2] = keep[long - 1]
    above[3] = keep[steps - 1]
    above[4] = gains[1]

    def added(terms):
        while len(terms) > 1:
            terms = [terms[k] + terms[k + 1] for k in range(0, len(terms), 2)]
        return terms[0]

    def group_at(there, i):
        return nz[there * steps + i // 2, (i % 2) * half : (i % 2 + 1) * half, :]

    def summed(there, carry):
        return carry + added(
            [omega[i, pl.ds(there, 1), :] * group_at(there, i) for i in range(long)]
        )

    carry_top = lax.fori_loop(chip + 1, chips, summed, jnp.zeros((half, modes), F32))
    carry_low = above[4, pl.ds(chip, 1), :] * carry_top + added(
        [above[5 + i, pl.ds(chip, 1), :] * group_at(chip, steps + i) for i in range(steps)]
    )
    kin_top = (above[2, pl.ds(chip, 1), :] * carry_top).astype(BF16)
    kin_low = (above[3, pl.ds(chip, 1), :] * carry_low).astype(BF16)
    slot = 2 * me_s + core

    out_low, out_top = kin.at[2 * ns], kin.at[2 * ns + 1]
    out_low[...] = kin_low
    out_top[...] = kin_top

    def low_to_plane(other):
        return pltpu.make_async_remote_copy(
            src_ref=out_low, dst_ref=kin.at[slot], send_sem=send.at[4], recv_sem=recv.at[4],
            device_id=(2 * chip, other), device_id_type=MESH,
        )

    def top_to_plane(other):
        return pltpu.make_async_remote_copy(
            src_ref=out_top, dst_ref=kin.at[slot], send_sem=send.at[4], recv_sem=recv.at[4],
            device_id=(2 * chip + 1, other), device_id_type=MESH,
        )

    all_copies(top_to_plane)
    all_copies(low_to_plane)

    @pl.when(core == 0)
    def _():
        top_to_plane(me_s).start()
        kin[slot] = kin_low

    @pl.when(core == 1)
    def _():
        low_to_plane(me_s).start()
        kin[slot] = kin_top

    noise_part(limits[3], total)

    wait_bytes(rows.at[0, pl.ds(0, ns - 1)], recv.at[2])
    loads[4].wait()
    halves = pltpu.make_async_remote_copy(
        src_ref=rows.at[core], dst_ref=rows.at[core], send_sem=send.at[6], recv_sem=recv.at[6],
        device_id=(sibling, me_s), device_id_type=MESH,
    )
    halves.start()

    wait_bytes(cs.at[pl.ds(0, (ns - 1) * long)], recv.at[1])
    wait_bytes(ps.at[pl.ds(0, ns - 1)], recv.at[3])
    c = [cs[pl.ds(i, ns, stride=long), :] for i in range(steps)]
    inv_s = cs[pl.ds(steps, ns, stride=long), :]
    pa, pb = ps[:, 0, :], ps[:, 1, :]
    now = pb + pa
    for i in range(steps):
        pa = pa * (c[i] * c[i])
        after = now + pa
        kept = now / after
        inner = kept * inv_s
        coef_s[i] = inner * lax.rsqrt(inner)
        if i < steps - 1:
            coef_a[i] = kept * c[i + 1]
        now = after

    halves.wait_recv()
    wait_bytes(kin.at[pl.ds(0, 2 * ns - 1)], recv.at[4])

    for b in range(ns):
        value = jnp.concatenate([kin[2 * b], kin[2 * b + 1]], axis=0).astype(F32)
        for i in range(steps - 1, -1, -1):
            if i < steps - 1:
                value = coef_a[i, pl.ds(b, 1), :] * value
            value = value + coef_s[i, pl.ds(b, 1), :] * nz[(chips + b) * steps + i]
            vals[b, pl.ds(i * vecs, vecs), :] = value.astype(BF16)
        product = lax.dot_general(
            jnp.concatenate([rows[0, b], rows[1, b]], axis=0), vals[b], (((1,), (1,)), ((), ())), preferred_element_type=F32
        )
        if b == 0:
            out_ref[...] = product
        else:
            out_ref[...] += product

    @pl.when(third)
    def _():
        wait_bytes(cz.at[pl.ds(0, (outer - 1) * steps)], send.at[0])

    @pl.when(jnp.logical_not(third))
    def _():
        wait_bytes(cz.at[pl.ds(0, (chips - 1) * steps)], send.at[0])

    @pl.when(chip == 0)
    def _():
        wait_bytes(cz.at[pl.ds(0, (chips - outer) * (outer - split) * steps)], send.at[7])

    wait_bytes(cs.at[pl.ds(0, (ns - 1) * long)], send.at[1])
    wait_bytes(rows.at[0, pl.ds(0, ns - 1)], send.at[2])
    halves.wait_send()
    wait_bytes(ps.at[pl.ds(0, ns - 1)], send.at[3])
    wait_bytes(kin.at[pl.ds(0, 2 * ns - 1)], send.at[4])
    across.wait_send()


def solution(mesh):
    zt, ns = mesh.shape["tm"], mesh.shape["space"]

    def local(spectrum, coupling, spatial_basis, noise_keys, noise_counters):
        steps, modes = coupling.shape
        vecs = noise_keys.shape[0]
        nodes = spatial_basis.shape[0] // ns
        vmem, smem = pltpu.VMEM, pltpu.SMEM
        return pl.pallas_call(
            functools.partial(kernel, zt, ns, steps, vecs),
            out_shape=jax.ShapeDtypeStruct((nodes, steps * vecs), F32),
            in_specs=[pl.BlockSpec(memory_space=pltpu.HBM)] * 5,
            out_specs=pl.BlockSpec(memory_space=vmem),
            scratch_shapes=[
                smem((vecs,), I32),
                smem((vecs,), I32),
                vmem((1, modes), F32),
                vmem((steps, modes), F32),
                vmem((2, vecs, modes), I32),
                vmem((2 * steps, modes), F32),
                vmem((zt * steps, modes), F32),
                vmem((2 * steps * ns, modes), F32),
                vmem((ns, 2, modes), F32),
                vmem((2, ns, nodes // 2, modes), BF16),
                vmem((2 * ns + 2, vecs // 2, modes), BF16),
                vmem((2, modes), F32),
                vmem(((zt // 2 + ns) * steps, vecs, modes), F32),
                vmem((2 * steps, zt // 2, modes), F32),
                vmem((5 + steps, zt // 2, modes), F32),
                vmem((steps, ns, modes), F32),
                vmem((steps, ns, modes), F32),
                vmem((ns, steps * vecs, modes), BF16),
                pltpu.SemaphoreType.DMA((8,)),
                pltpu.SemaphoreType.DMA((8,)),
                pltpu.SemaphoreType.DMA((5,)),
                pltpu.SemaphoreType.REGULAR((5,)),
            ],
            compiler_params=pltpu.CompilerParams(
                collective_id=0, has_side_effects=True, vmem_limit_bytes=62 * 2**20
            ),
        )(noise_keys, noise_counters, spectrum.reshape(1, modes), coupling, spatial_basis)

    return jax.shard_map(
        local,
        mesh=mesh,
        in_specs=(P("space"), P("tm", "space"), P(None, "space"), P(), P()),
        out_specs=P("space", "tm"),
        check_vma=False,
    )
```
